128 devices in a mesh: row: 32 (over z, y, core), col: 4 (over x).
Axes of the slice: x: 4, y: 4, z: 4, core: 2. Of those that a mesh axis runs over, the one named last changes fastest.
Arguments:
- trailing: float32 [16384, 16384], P('row', 'col'), may hold values from -40 to 40, as said below
Outputs:
- reduced: float32 [16384, 16384], P('row', 'col')
- reflectors: float32 [16384, 64], P('row')
The draws below stay inside these ranges and needn't reach their ends.
Inputs may be any that keep to these rules, and one draw needn't show every extreme that they name: symmetric: trailing equals its transpose.
All inputs are finite; a program needn't handle non-finite values.
Results may differ from the reference program's by a relative error of at most 0.0003.
Values sent between devices are 32-bit elements; how exact they have to be, the bound alone decides.
A program may use at most 128 MiB of HBM per device.

```python
import jax
import jax.numpy as jnp
from jax import lax

N = 16384
NB = 64


def draw_trailing(key, part):
    key = jax.random.fold_in(key, 11)
    first, second = jax.random.split(key, 2)
    diagonal = jax.random.uniform(second, (N,), jnp.float32, 1.0, 4.0)
    base = jax.random.normal(first, (N, N), jnp.float32)
    symmetric = (base + base.T) * 0.7071
    return symmetric + jnp.diag(diagonal)


def setup_inputs(seed: int = 0) -> dict:
    key_of = jax.random.split(jax.random.key(seed), 2)
    return {
        "trailing": draw_trailing(jax.random.fold_in(key_of[1], 71), 0),
    }


highest = lax.Precision.HIGHEST

def reflect_column(step_col, col_dots, pivot_row, panel_cols, row_ids):
    width = panel_cols.shape[1]
    norm_sq = col_dots[step_col]
    leading = pivot_row[step_col]
    length = jnp.sqrt(norm_sq)
    reflected = jnp.where(leading >= 0.0, -length, length)
    factor = (reflected - leading) / reflected
    scaling = 1.0 / (leading - reflected)
    active = row_ids >= NB + step_col
    on_pivot = row_ids == NB + step_col
    current = lax.dynamic_slice_in_dim(panel_cols, step_col, 1, 1)[:, 0]
    masked_col = jnp.where(active, current, 0.0)
    vector = jnp.where(on_pivot, 1.0, masked_col * scaling)
    products = (col_dots - reflected * pivot_row) * scaling
    columns = jnp.arange(width)
    later = jnp.where(columns > step_col, products, 0.0)
    panel_cols = panel_cols - factor * vector[:, None] * later[None, :]
    new_column = jnp.where(active, jnp.where(on_pivot, reflected, 0.0), current)
    panel_cols = jnp.where((columns == step_col)[None, :], new_column[:, None], panel_cols)
    return (panel_cols, vector, factor)

def block_factor(gram_refl, factors):
    width = gram_refl.shape[0]
    columns = jnp.arange(width)

    def turn(step_col, block):
        factor = factors[step_col]
        prior = lax.dynamic_slice_in_dim(gram_refl, step_col, 1, 1)[:, 0]
        prior = jnp.where(columns < step_col, prior, 0.0)
        column = -factor * jnp.dot(block, prior, precision=highest)
        column = jnp.where(columns == step_col, factor, column)
        return jnp.where((columns == step_col)[None, :], column[:, None], block)
    return lax.fori_loop(0, width, turn, jnp.zeros((width, width), jnp.float32))

def reference(trailing):
    row_ids = jnp.arange(N)
    columns = jnp.arange(NB)

    def turn(step_col, carry):
        panel_cols, vectors, factors = carry
        active = row_ids >= NB + step_col
        current = lax.dynamic_slice_in_dim(panel_cols, step_col, 1, 1)[:, 0]
        col_dots = jnp.dot(jnp.where(active, current, 0.0), panel_cols, precision=highest)
        pivot_row = lax.dynamic_slice_in_dim(panel_cols, NB + step_col, 1, 0)[0]
        panel_cols, vector, factor = reflect_column(step_col, col_dots, pivot_row, panel_cols, row_ids)
        vectors = jnp.where((columns == step_col)[None, :], vector[:, None], vectors)
        factors = jnp.where(columns == step_col, factor, factors)
        return (panel_cols, vectors, factors)
    start = (trailing[:, :NB], jnp.zeros((N, NB), jnp.float32), jnp.zeros((NB,), jnp.float32))
    panel_cols, vectors, factors = lax.fori_loop(0, NB, turn, start)
    gram_refl = jnp.dot(vectors.T, vectors, precision=highest)
    block = block_factor(gram_refl, factors)
    product = jnp.dot(trailing, vectors, precision=highest)
    corner = jnp.dot(vectors.T, product, precision=highest)
    small = jnp.dot(jnp.dot(block.T, corner, precision=highest), block, precision=highest)
    update = jnp.dot(product, block, precision=highest) - 0.5 * jnp.dot(vectors, small, precision=highest)
    reduced = trailing - jnp.dot(vectors, update.T, precision=highest) - jnp.dot(update, vectors.T, precision=highest)
    return (reduced, vectors)
```

```python
import functools

import jax
import jax.numpy as jnp
from jax import lax
from jax.experimental import pallas as pl
from jax.experimental.pallas import tpu as pltpu
from jax.sharding import PartitionSpec as P

NB = 64
SIDE = 4
MESH = pl.DeviceIdType.MESH
HIGHEST = lax.Precision.HIGHEST
NN = (((1,), (0,)), ((), ()))
NT = (((1,), (1,)), ((), ()))


def dot(a, b, dims=NN):
    return lax.dot_general(a, b, dims, precision=HIGHEST, preferred_element_type=jnp.float32)


def dot16(a, b, dims=NN):
    return lax.dot_general(a, b, dims, preferred_element_type=jnp.float32)


def split(a):
    high = a.astype(jnp.bfloat16)
    return high, (a - high.astype(jnp.float32)).astype(jnp.bfloat16)


def wrap(i):
    return lax.rem(i, SIDE)


class Ids:
    def __init__(self):
        self.count = 0

    def take(self, n):
        first = self.count
        self.count += n
        return first


IDS = Ids()
HOME = IDS.take(4)
ROWS = IDS.take(4)
GATHER_P = IDS.take(20)
GATHER_Y = IDS.take(20)
GRAM = IDS.take(4)
CORNER = IDS.take(4)
REDUCE = IDS.take(4)
YROWS = IDS.take(4)
COUNT = IDS.count


def factor(gt, r_ref):
    lanes = lax.broadcasted_iota(jnp.int32, (8, 128), 1)
    subs = lax.broadcasted_iota(jnp.int32, (8, 128), 0)
    square = jnp.concatenate([gt, jnp.zeros_like(gt)], axis=0)
    t_all = jnp.transpose(square)[NB:, :]
    S, T, C = [], [], []
    for b in range(8):
        rows = slice(8 * b, 8 * b + 8)
        unit = jnp.where(lanes == subs + (8 * b + NB), 1.0, 0.0)
        S.append(jnp.where(lanes < NB, gt[rows], unit))
        T.append(jnp.where(lanes < NB, t_all[rows], unit))
        C.append(jnp.where(lanes == subs + 8 * b, 1.0, 0.0))
    lane_row = lax.broadcasted_iota(jnp.int32, (1, 128), 1)
    for j in range(NB):
        b, s = j // 8, j % 8
        srow, trow = S[b][s : s + 1, :], T[b][s : s + 1, :]
        d, a = srow[:, j : j + 1], trow[:, j : j + 1]
        length = jnp.sqrt(d)
        lead = jnp.where(a >= 0.0, -length, length)
        rrow = jnp.where(lane_row >= j, srow, 0.0) * (1.0 / lead)
        r_ref[NB + j : NB + j + 1, :] = rrow
        urow = jnp.where(lane_row < NB, jnp.where(lane_row >= j, trow - rrow, 0.0), trow)
        pivot_inv = 1.0 / (a - lead)
        d_inv = 1.0 / d
        later = lane_row > j
        surow = jnp.where(later, srow, 0.0) * d_inv
        turow = jnp.where(later, urow, 0.0) * pivot_inv
        for m in range(b, 8):
            scol, tcol = S[m][:, j : j + 1], T[m][:, j : j + 1]
            ds, dt = scol * surow, tcol * turow
            if m == b:
                ds, dt = jnp.where(subs > s, ds, 0.0), jnp.where(subs > s, dt, 0.0)
            S[m] = S[m] - ds
            T[m] = T[m] - dt
        for m in range(b + 1):
            ccol = C[m][:, j : j + 1]
            C[m] = jnp.where(lanes == j, ccol * pivot_inv, C[m] - ccol * jnp.where(lane_row < NB, turow, 0.0))
    return jnp.concatenate(C, axis=0), jnp.concatenate(T, axis=0)


def kernel(
    a_hbm, x_out, z_out,
    a_v, head, head_t, pbuf, ybuf, prow, yrow, part, rbuf, gbuf, cbuf, r_ref, h_ref,
    load_sem, send, recv,
):
    r, x = lax.axis_index("row"), lax.axis_index("col")
    z, y, k = r // 8, lax.rem(r // 2, SIDE), lax.rem(r, 2)
    lanes64 = lax.broadcasted_iota(jnp.int32, (NB, 128), 1)

    def dev(z_, y_, k_, x_):
        return (z_ * 8 + y_ * 2 + k_, x_)

    def remote(src, dst, s, t, device):
        return pltpu.make_async_remote_copy(
            src_ref=src, dst_ref=dst, send_sem=send.at[s], recv_sem=recv.at[t],
            device_id=device, device_id_type=MESH,
        )

    sibling = dev(z, y, 1 - k, x)
    whole = pltpu.make_async_copy(a_hbm, a_v, load_sem.at[0])
    first = pltpu.make_async_copy(a_hbm.at[:, pl.ds(0, 128)], head, load_sem.at[1])
    owns = x == 0

    @pl.when(owns)
    def _():
        first.start()

    whole.start()

    barrier = pltpu.get_barrier_semaphore()
    peers = [dev(wrap(z + i), y, k, wrap(x + j)) for i in range(SIDE) for j in range(SIDE) if i or j]
    peers += [dev(z, wrap(y + i), k, x) for i in range(1, SIDE)] + [sibling]
    for peer in peers:
        pl.semaphore_signal(barrier, inc=1, device_id=peer, device_id_type=MESH)

    r_ref[0:NB, :] = jnp.zeros((NB, 128), jnp.float32)

    @pl.when(owns)
    def _():
        first.wait()
        head_t[...] = jnp.transpose(head[...])

        @pl.when(r == 0)
        def _():
            head_t[0:NB, 0:128] = jnp.where(lanes64 >= NB, head_t[0:NB, 0:128], 0.0)

    pl.semaphore_wait(barrier, len(peers))

    def home_piece(q):
        return head_t.at[pl.ds(0, NB), pl.ds(q * 128, 128)]

    def home_copy(q):
        return remote(home_piece(q), pbuf.at[k, y, q], HOME + q, HOME, dev(q, y, k, z))

    self_home = owns & (r // 8 == 0)
    local_home = pltpu.make_async_copy(home_piece(0), pbuf.at[k, y, 0], load_sem.at[2])

    def rows_copy(d):
        return remote(head_t.at[pl.ds(0, NB)], prow, ROWS + d, ROWS, dev(z, y, k, d))

    local_rows = pltpu.make_async_copy(head_t.at[pl.ds(0, NB)], prow, load_sem.at[3])

    @pl.when(owns)
    def _():
        @pl.when(z == 0)
        def _():
            local_home.start()

        @pl.when(z != 0)
        def _():
            home_copy(0).start()

        for q in range(1, SIDE):
            home_copy(q).start()
        for d in range(1, SIDE):
            rows_copy(d).start()
        local_rows.start()

    @pl.when(self_home)
    def _():
        local_home.wait()

    @pl.when(jnp.logical_not(self_home))
    def _():
        remote(pbuf.at[k, y, z], pbuf.at[k, y, z], HOME, HOME, sibling).wait_recv()

    low, high = pl.ds(0, NB // 2), pl.ds(NB // 2, NB // 2)

    def gather(buf, base):
        sends = []

        def go(src, slot, device):
            copy = remote(src, src, base + slot, base + slot, device)
            copy.start()
            sends.append(copy)

        def came(dst, slot):
            remote(dst, dst, base + slot, base + slot, sibling).wait_recv()

        for d in range(1, SIDE):
            go(buf.at[k, y, z, low], d - 1, dev(wrap(z + d), y, k, x))
            go(buf.at[k, y, z, high], 3 + d - 1, dev(z, wrap(y + d), k, x))
        for d in range(1, SIDE):
            came(buf.at[k, y, wrap(z + SIDE - d), low], d - 1)
        for d in range(1, SIDE):
            go(buf.at[k, y, :, low], 6 + d - 1, dev(z, wrap(y + d), k, x))
        for d in range(1, SIDE):
            came(buf.at[k, wrap(y + SIDE - d), z, high], 3 + d - 1)
        for d in range(1, SIDE):
            go(buf.at[k, :, z, high], 9 + d - 1, dev(wrap(z + d), y, k, x))
        go(buf.at[k, y, :, low], 12, sibling)
        go(buf.at[k, :, z, high], 16, sibling)
        for d in range(1, SIDE):
            came(buf.at[k, wrap(y + SIDE - d), :, low], 6 + d - 1)
            go(buf.at[k, wrap(y + SIDE - d), :, low], 12 + d, sibling)
            came(buf.at[k, :, wrap(z + SIDE - d), high], 9 + d - 1)
            go(buf.at[k, :, wrap(z + SIDE - d), high], 16 + d, sibling)
        for d in range(SIDE):
            came(buf.at[1 - k, wrap(y + SIDE - d), :, low], 12 + d)
            came(buf.at[1 - k, :, wrap(z + SIDE - d), high], 16 + d)
        return sends

    sends = gather(pbuf, GATHER_P)

    def wide(buf, m):
        return jnp.concatenate([buf[m % 2, m // 2, q] for q in range(SIDE)], axis=1)

    gram = jnp.zeros((NB, NB), jnp.float32)
    for m in range(8):
        piece = wide(pbuf, m)
        gram = gram + dot(piece, piece, NT)
    top = jnp.where(owns, pbuf[0, 0, 0], 0.0)
    gbuf[x] = jnp.where(lanes64 < NB, jnp.concatenate([gram, gram], axis=1), top)

    def exchange(buf, base):
        for d in range(1, SIDE):
            copy = remote(buf.at[x], buf.at[x], base + d, base + d, dev(z, y, k, wrap(x + d)))
            copy.start()
            sends.append(copy)

    def exchanged(buf, base):
        for d in range(1, SIDE):
            there = buf.at[wrap(x + SIDE - d)]
            remote(there, there, base + d, base + d, sibling).wait_recv()
        return (buf[0] + buf[1]) + (buf[2] + buf[3])

    exchange(gbuf, GRAM)

    whole.wait()
    acc = jnp.zeros((2 * NB, a_v.shape[0]), jnp.float32)
    for m in range(8):
        p_hi, p_lo = split(wide(pbuf, m))
        both = jnp.concatenate([p_hi, p_lo], axis=0)
        a_hi, a_lo = split(a_v[:, m * 512 : (m + 1) * 512])
        acc = acc + (dot16(both, a_hi, NT) + dot16(both, a_lo, NT))
    part[...] = acc[:NB] + acc[NB:]

    gt = exchanged(gbuf, GRAM)
    m_all, t_all = factor(gt, r_ref)
    m_t = jnp.transpose(jnp.concatenate([m_all, jnp.zeros_like(m_all)], axis=0))[:NB, :]
    r_all = r_ref[...]
    r_shift = jnp.transpose(r_all)[:NB, :]
    k_t = -dot(t_all[:, NB:], r_all[NB:, NB:])

    @pl.when(owns)
    def _():
        part[...] = part[...] - dot(r_shift[:, NB:], head_t[NB : 2 * NB, :])

    def piece_of(q):
        return part.at[:, pl.ds(pl.multiple_of(q * 128, 128), 128)]

    def reduce_copy(d):
        q = wrap(z + d)
        return remote(piece_of(q), rbuf.at[x], REDUCE + d, REDUCE + x, dev(q, y, k, z))

    diagonal = x == z
    local_reduce = pltpu.make_async_copy(piece_of(z), rbuf.at[x], load_sem.at[4])

    @pl.when(diagonal)
    def _():
        local_reduce.start()

    @pl.when(jnp.logical_not(diagonal))
    def _():
        reduce_copy(0).start()

    for d in range(1, SIDE):
        reduce_copy(d).start()

    def reduce_came(d):
        there = rbuf.at[wrap(x + d)]
        remote(there, there, REDUCE, REDUCE + wrap(x + d), sibling).wait_recv()

    for d in range(1, SIDE):
        reduce_came(d)

    @pl.when(diagonal)
    def _():
        local_reduce.wait()

    @pl.when(jnp.logical_not(diagonal))
    def _():
        reduce_came(0)

    ybuf[k, y, z] = (rbuf[0] + rbuf[1]) + (rbuf[2] + rbuf[3])

    def yrows_copy(d):
        return remote(ybuf.at[k, y, z], yrow.at[z], YROWS + d, YROWS + z, dev(x, y, k, wrap(x + d)))

    local_yrows = pltpu.make_async_copy(ybuf.at[k, y, z], yrow.at[z], load_sem.at[5])

    @pl.when(diagonal)
    def _():
        local_yrows.start()

    @pl.when(jnp.logical_not(diagonal))
    def _():
        yrows_copy(0).start()

    for d in range(1, SIDE):
        yrows_copy(d).start()

    sends += gather(ybuf, GATHER_Y)

    shift_c = jnp.where(owns, r_shift, 0.0)
    corner = jnp.zeros((NB, NB), jnp.float32)
    for m in range(8):
        piece = wide(pbuf, m)
        if m == 0:
            piece = jnp.concatenate([piece[:, :128] - shift_c, piece[:, 128:]], axis=1)
        corner = corner + dot(piece, wide(ybuf, m), NT)
    cbuf[x] = jnp.concatenate([corner, jnp.zeros_like(corner)], axis=1)
    exchange(cbuf, CORNER)
    corner = exchanged(cbuf, CORNER)[:, :NB]
    small = dot(dot(k_t, corner), k_t, NT)
    mt = m_t[:, :NB]
    zero = jnp.zeros((NB, NB), jnp.float32)
    h_ref[:NB, :] = jnp.concatenate([-0.5 * dot(small, mt), k_t], axis=1)
    h_ref[NB:, :] = jnp.concatenate([mt, zero], axis=1)
    h = h_ref[...]

    for m in range(8):
        piece = wide(pbuf, m)
        if m == 0:
            piece = jnp.concatenate([piece[:, :128] - shift_c, piece[:, 128:]], axis=1)
        both = jnp.concatenate([piece, wide(ybuf, m)], axis=0)
        z_out[:, m * 512 : (m + 1) * 512] = dot(h, both)

    for d in range(1, SIDE):
        q = wrap(z + d)
        remote(yrow.at[q], yrow.at[q], YROWS, YROWS + q, sibling).wait_recv()

    @pl.when(diagonal)
    def _():
        local_yrows.wait()

    @pl.when(jnp.logical_not(diagonal))
    def _():
        remote(yrow.at[z], yrow.at[z], YROWS, YROWS + z, sibling).wait_recv()

    @pl.when(owns)
    def _():
        local_rows.wait()

    @pl.when(jnp.logical_not(owns))
    def _():
        remote(prow, prow, ROWS, ROWS, sibling).wait_recv()

    piece = prow[...]
    shift_r = jnp.where(r == 0, r_shift, 0.0)
    piece = jnp.concatenate([piece[:, :128] - shift_r, piece[:, 128:]], axis=1)
    both = jnp.concatenate([piece] + [jnp.concatenate([yrow[q] for q in range(SIDE)], axis=1)], axis=0)
    uv = dot(h, both)
    x_out[...] = jnp.transpose(jnp.concatenate([uv[NB:], uv[:NB]], axis=0))

    @pl.when(owns)
    def _():
        @pl.when(z != 0)
        def _():
            home_copy(0).wait_send()

        for q in range(1, SIDE):
            home_copy(q).wait_send()
        for d in range(1, SIDE):
            rows_copy(d).wait_send()

    @pl.when(jnp.logical_not(diagonal))
    def _():
        reduce_copy(0).wait_send()
        yrows_copy(0).wait_send()

    for d in range(1, SIDE):
        reduce_copy(d).wait_send()
        yrows_copy(d).wait_send()
    for copy in sends:
        copy.wait_send()


def update_kernel(a_ref, x_ref, z_ref, out_ref, v_ref):
    x_hi, x_lo = split(x_ref[...])
    z_hi, z_lo = split(z_ref[...])
    out_ref[...] = a_ref[...] - ((dot16(x_lo, z_hi) + dot16(x_hi, z_lo)) + dot16(x_hi, z_hi))
    v_ref[...] = x_ref[:, :NB]


def local(trailing):
    rows, cols = trailing.shape
    f32 = jnp.float32
    x_mat, z_mat = pl.pallas_call(
        kernel,
        out_shape=(jax.ShapeDtypeStruct((rows, 128), f32), jax.ShapeDtypeStruct((128, cols), f32)),
        in_specs=[pl.BlockSpec(memory_space=pl.ANY)],
        out_specs=(pl.BlockSpec(memory_space=pltpu.VMEM), pl.BlockSpec(memory_space=pltpu.VMEM)),
        scratch_shapes=[
            pltpu.VMEM((rows, cols), f32),
            pltpu.VMEM((rows, 128), f32),
            pltpu.VMEM((128, rows), f32),
            pltpu.VMEM((2, SIDE, SIDE, NB, 128), f32),
            pltpu.VMEM((2, SIDE, SIDE, NB, 128), f32),
            pltpu.VMEM((NB, rows), f32),
            pltpu.VMEM((SIDE, NB, 128), f32),
            pltpu.VMEM((NB, rows), f32),
            pltpu.VMEM((SIDE, NB, 128), f32),
            pltpu.VMEM((SIDE, NB, 128), f32),
            pltpu.VMEM((SIDE, NB, 128), f32),
            pltpu.VMEM((128, 128), f32),
            pltpu.VMEM((128, 128), f32),
            pltpu.SemaphoreType.DMA((6,)),
            pltpu.SemaphoreType.DMA((COUNT,)),
            pltpu.SemaphoreType.DMA((COUNT,)),
        ],
        compiler_params=pltpu.CompilerParams(
            collective_id=0, has_side_effects=True, vmem_limit_bytes=40 * 2**20
        ),
    )(trailing)
    step = 64
    return pl.pallas_call(
        update_kernel,
        grid=(rows // step,),
        out_shape=(jax.ShapeDtypeStruct((rows, cols), f32), jax.ShapeDtypeStruct((rows, NB), f32)),
        in_specs=[
            pl.BlockSpec((step, cols), lambda i: (i, 0)),
            pl.BlockSpec((step, 128), lambda i: (i, 0)),
            pl.BlockSpec((128, cols), lambda i: (0, 0)),
        ],
        out_specs=(pl.BlockSpec((step, cols), lambda i: (i, 0)), pl.BlockSpec((step, NB), lambda i: (i, 0))),
        compiler_params=pltpu.CompilerParams(vmem_limit_bytes=40 * 2**20),
    )(trailing, x_mat, z_mat)


def solution(mesh):
    return jax.shard_map(
        local, mesh=mesh, in_specs=(P("row", "col"),), out_specs=(P("row", "col"), P("row", None)), check_vma=False
    )
```

```python
import jax
import jax.numpy as jnp
from jax import lax
from jax.experimental import pallas as pl
from jax.experimental.pallas import tpu as pltpu
from jax.sharding import PartitionSpec as P

NB = 64
SIDE = 4
MESH = pl.DeviceIdType.MESH
HIGHEST = lax.Precision.HIGHEST
NN = (((1,), (0,)), ((), ()))
NT = (((1,), (1,)), ((), ()))
TN = (((0,), (0,)), ((), ()))


def dot(a, b, dims=NN):
    return lax.dot_general(a, b, dims, precision=HIGHEST, preferred_element_type=jnp.float32)


def dot16(a, b, dims=NN):
    return lax.dot_general(a, b, dims, preferred_element_type=jnp.float32)


def split(a):
    high = a.astype(jnp.bfloat16)
    return high, (a - high.astype(jnp.float32)).astype(jnp.bfloat16)


def split3(a):
    high = a.astype(jnp.bfloat16)
    rest = a - high.astype(jnp.float32)
    middle = rest.astype(jnp.bfloat16)
    return high, middle, (rest - middle.astype(jnp.float32)).astype(jnp.bfloat16)


def stack(parts):
    return jnp.concatenate(parts, axis=0)


def wrap(i):
    return lax.rem(i, SIDE)


AROUND = [(2, 2), (2, 1), (2, 3), (1, 2), (3, 2), (1, 1), (3, 3), (1, 3), (3, 1), (2, 0), (0, 2), (1, 0), (3, 0), (0, 1), (0, 3)]


class Ids:
    def __init__(self):
        self.count = 0

    def take(self, n):
        first = self.count
        self.count += n
        return first


IDS = Ids()
ROWS = IDS.take(4)
HOME = IDS.take(4)
GRAM = IDS.take(4)
SPREAD = IDS.take(17)
HALVES = IDS.take(4)
SCATTER = IDS.take(16)
GATHER = IDS.take(20)
OWN_ROWS = IDS.take(4)
CORNER = IDS.take(4)
COUNT = IDS.count


def factor(gt, r_ref, u_ref, out):
    lanes = lax.broadcasted_iota(jnp.int32, (8, 128), 1)
    subs = lax.broadcasted_iota(jnp.int32, (8, 128), 0)
    lane = lax.broadcasted_iota(jnp.int32, (1, 128), 1)
    t_all = jnp.transpose(stack([gt, jnp.zeros_like(gt)]))[NB:, :]
    S, T, C = [], [], []
    for b in range(8):
        rows = slice(8 * b, 8 * b + 8)
        unit = jnp.where(lanes == subs + (8 * b + NB), 1.0, 0.0)
        S.append(jnp.where(lanes < NB, gt[rows], unit))
        T.append(jnp.where(lanes < NB, t_all[rows], unit))
        C.append(jnp.where(lanes == subs + 8 * b, 1.0, 0.0))
    for j in range(NB):
        b, s = j // 8, j % 8
        srow, trow = S[b][s : s + 1, :], T[b][s : s + 1, :]
        d = jnp.broadcast_to(srow[:, j : j + 1], (1, 128))
        a = jnp.broadcast_to(trow[:, j : j + 1], (1, 128))
        root_inv = lax.rsqrt(d)
        positive = a >= 0.0
        pivot_inv = 1.0 / (jnp.abs(a) + d * root_inv)
        pivot_inv = jnp.where(positive, pivot_inv, -pivot_inv)
        rrow = jnp.where(lane >= j, srow, 0.0) * jnp.where(positive, -root_inv, root_inv)
        r_ref[NB + j : NB + j + 1, :] = rrow
        urow = jnp.where(lane < NB, jnp.where(lane >= j, trow - rrow, 0.0), trow)
        u_ref[j : j + 1, :] = urow
        later = lane > j
        surow = jnp.where(later, srow, 0.0) * (1.0 / d)
        turow = jnp.where(later, urow, 0.0) * pivot_inv
        for m in range(b, 8):
            scol, tcol = S[m][:, j : j + 1], T[m][:, j : j + 1]
            if m == b:
                below = subs[:, :1] > s
                scol, tcol = jnp.where(below, scol, 0.0), jnp.where(below, tcol, 0.0)
            S[m] = S[m] - scol * surow
            T[m] = T[m] - tcol * turow
        curow = jnp.where(lane < NB, jnp.where(lane == j, 1.0 - pivot_inv, turow), 0.0)
        for m in range(b + 1):
            C[m] = C[m] - C[m][:, j : j + 1] * curow
        if s == 7:
            if b == 7:
                out += [stack(C), stack(T)]
            yield


def kernel(
    a_hbm, a_v, x_out, z_out, vt_out,
    a_hi, a_lo, head, lead, panel, prow, pq, dbuf, sbuf, rbuf, wv, wv_rows, gbuf, gt_ref, cbuf, r_ref, u_ref,
    load_sem, send, recv,
):
    r, x = lax.axis_index("row"), lax.axis_index("col")
    z, y, k = r // 8, lax.rem(r // 2, SIDE), lax.rem(r, 2)
    lanes64 = lax.broadcasted_iota(jnp.int32, (NB, 128), 1)

    def dev(z_, y_, k_, x_):
        return (z_ * 8 + y_ * 2 + k_, x_)

    def remote(src, dst, s, t, device):
        return pltpu.make_async_remote_copy(
            src_ref=src, dst_ref=dst, send_sem=send.at[s], recv_sem=recv.at[t],
            device_id=device, device_id_type=MESH,
        )

    sends = []

    def launch(copy, when=None):
        if when is None:
            copy.start()
        else:
            pl.when(when)(copy.start)
        sends.append((copy, when))

    def finish():
        for copy, when in sends:
            if when is None:
                copy.wait_send()
            else:
                pl.when(when)(copy.wait_send)
        sends.clear()

    sibling = dev(z, y, 1 - k, x)

    def came(dst, slot):
        remote(dst, dst, slot, slot, sibling).wait_recv()

    owns = x == 0
    first_row = r == 0
    half = a_v.shape[0] // 2

    def head_load(q):
        rows = pl.ds(q * 128, 128)
        return pltpu.make_async_copy(a_hbm.at[rows, pl.ds(0, 128)], head.at[rows], load_sem.at[q])

    def load(i):
        rows = pl.ds(i * half, half)
        return pltpu.make_async_copy(a_hbm.at[rows], a_v.at[rows], load_sem.at[4 + i])

    lead_load = pltpu.make_async_copy(a_hbm.at[pl.ds(0, NB)], lead, load_sem.at[6])

    @pl.when(owns)
    def _():
        for q in range(SIDE):
            head_load(q).start()

    pl.when(first_row)(lead_load.start)
    barrier = pltpu.get_barrier_semaphore()
    peers = [dev(wrap(z + i), y, k, wrap(x + j)) for i in range(SIDE) for j in range(1, SIDE)]
    peers += [dev(wrap(z + i), wrap(y + j), k, x) for i, j in AROUND] + [sibling]
    for peer in peers:
        pl.semaphore_signal(barrier, inc=1, device_id=peer, device_id_type=MESH)

    load(0).start()
    load(1).start()
    r_ref[0:NB, :] = jnp.zeros((NB, 128), jnp.float32)

    @pl.when(owns)
    def _():
        for q in range(SIDE):
            head_load(q).wait()
            panel[q] = jnp.transpose(head[q * 128 : (q + 1) * 128, :])
            if q == 0:
                panel[0, 0:NB] = jnp.where(first_row & (lanes64 < NB), 0.0, panel[0, 0:NB])
            prow[:, q * 128 : (q + 1) * 128] = panel[q, 0:NB]

    pl.semaphore_wait(barrier, len(peers))

    for d in (2, 1, 3):
        launch(remote(prow, prow, ROWS + d, ROWS, dev(z, y, k, d)), owns)

    def home_copy(q):
        return remote(panel.at[q], pq, HOME + q, HOME, dev(q, y, k, z))

    self_home = owns & (z == 0)
    home_local = pltpu.make_async_copy(panel.at[0], pq, load_sem.at[7])
    pl.when(self_home)(home_local.start)
    launch(home_copy(0), owns & (z != 0))
    for q in range(1, SIDE):
        launch(home_copy(q), owns)

    def exchange(buf, base, when=None):
        for d in (2, 1, 3):
            launch(remote(buf.at[x], buf.at[x], base + d, base + d, dev(z, y, k, wrap(x + d))), when)

    def exchanged(buf, base):
        for d in range(1, SIDE):
            came(buf.at[wrap(x + SIDE - d)], base + d)
        return (buf[0] + buf[1]) + (buf[2] + buf[3])

    @pl.when(first_row)
    def _():
        lead_load.wait()
        lead[:, 0:128] = jnp.where(owns & (lanes64 < NB), 0.0, lead[:, 0:128])
        gram = jnp.zeros((3 * NB, 3 * NB), jnp.float32)
        for m in range(8):
            three = stack(split3(lead[:, m * 512 : (m + 1) * 512]))
            gram = gram + dot16(three, three, NT)
        gram = gram[:NB] + gram[NB : 2 * NB] + gram[2 * NB :]
        gram = gram[:, :NB] + gram[:, NB : 2 * NB] + gram[:, 2 * NB :]
        top = jnp.where(owns, lead[:, 0:128], 0.0)
        gbuf[x] = jnp.where(lanes64 < NB, jnp.concatenate([gram, gram], axis=1), top)

    exchange(gbuf, GRAM, first_row)

    def split_rows(part_id):
        load(part_id).wait()

        def body(step, carry):
            rows = pl.ds(pl.multiple_of(part_id * half + step * 16, 16), 16)
            for kk in range(2):
                for i in range(SIDE):
                    first = i * 1024 + kk * 512
                    a_hi[kk, i, rows, :], a_lo[kk, i, rows, :] = split(a_v[rows, first : first + 512])
            return carry

        lax.fori_loop(0, half // 16, body, 0)

    split_rows(0)
    split_rows(1)

    @pl.when(first_row)
    def _():
        gt_ref[...] = exchanged(gbuf, GRAM)

    launch(remote(gt_ref, gt_ref, SPREAD + 16, SPREAD, sibling), first_row)
    first_chip = (z == 0) & (y == 0)

    def gt_came():
        came(gt_ref, SPREAD)

    pl.when(first_chip & (k == 1))(gt_came)
    for i, j in AROUND:
        launch(remote(gt_ref, gt_ref, SPREAD + 4 * i + j, SPREAD, dev(wrap(z + i), wrap(y + j), k, x)), first_chip)

    pl.when(jnp.logical_not(owns))(remote(prow, prow, ROWS, ROWS, sibling).wait_recv)
    both = stack(split(prow[...]))

    def multiply(kk, i):
        new = dot16(both, a_hi[kk, i]) + dot16(both, a_lo[kk, i])
        return new[:NB] + new[NB:]

    for i in range(SIDE):
        new = multiply(1 - k, i)
        for q in range(SIDE):
            dbuf[1 - k, i, q] = new[:, q * 128 : (q + 1) * 128]
        launch(remote(dbuf.at[1 - k, i], sbuf.at[i], HALVES + i, HALVES + i, sibling))

    for i in range(SIDE):
        j = wrap(y + i)
        new = multiply(k, j)
        came(sbuf.at[j], HALVES + j)
        for q in range(SIDE):
            dbuf[k, j, q] = new[:, q * 128 : (q + 1) * 128] + sbuf[j, q]
        for h in (2, 1, 3, 0):
            if h or i:
                q = wrap(z + h)
                slot = SCATTER + 4 * h + i
                launch(remote(dbuf.at[k, j, q], rbuf.at[4 * h + i], slot, slot, dev(q, j, k, x)))

    pl.when(jnp.logical_not(first_chip))(gt_came)
    factors = []
    for _ in factor(gt_ref[...], r_ref, u_ref, factors):
        pass
    m_all, t_all = factors
    mt = jnp.transpose(stack([m_all, jnp.zeros_like(m_all)]))[:NB, :NB]
    r_all = r_ref[...]
    r_shift = jnp.transpose(r_all)[:NB, :]
    l_inv = t_all[:, NB:]
    k_t = -dot(l_inv, r_all[NB:, NB:])

    pl.when(self_home)(home_local.wait)
    pl.when(jnp.logical_not(self_home))(remote(pq, pq, HOME, HOME, sibling).wait_recv)
    piece = pq[0:NB] - jnp.where(first_row & owns, r_shift, 0.0)
    early = stack([dot(l_inv, pq[NB : 2 * NB]), dot(mt, piece)])
    total = dbuf[k, y, z]
    for slot in range(1, 16):
        came(rbuf.at[slot], SCATTER + slot)
        total = total + rbuf[slot]
    wv[k, y, z] = early + stack([dot(k_t, total), jnp.zeros_like(total)])

    for i, j in AROUND:
        slot = GATHER + 4 * i + j
        launch(remote(wv.at[k, y, z], wv.at[k, y, z], slot, slot, dev(wrap(z + i), wrap(y + j), k, x)))

    diagonal = x == z
    rows_local = pltpu.make_async_copy(wv.at[k, y, z], wv_rows.at[z], load_sem.at[8])

    def rows_copy(d):
        return remote(wv.at[k, y, z], wv_rows.at[z], OWN_ROWS + d, OWN_ROWS + z, dev(x, y, k, wrap(x + d)))

    pl.when(diagonal)(rows_local.start)
    launch(rows_copy(0), jnp.logical_not(diagonal))
    for d in (2, 1, 3):
        launch(rows_copy(d))
    b_t = dot(k_t, u_ref[:, :NB], NT)

    def gathered(j):
        for i in (0, 1, 3, 2):
            if i or j:
                came(wv.at[k, wrap(y + SIDE - j), wrap(z + SIDE - i)], GATHER + i * SIDE + j)
        there = wv.at[k, wrap(y + SIDE - j)]
        launch(remote(there, there, GATHER + 16 + j, GATHER + 16 + j, sibling))

    def sibling_came(j):
        came(wv.at[1 - k, wrap(y + SIDE - j)], GATHER + 16 + j)

    corner = [jnp.zeros((2 * NB, 2 * NB), jnp.float32)]

    def use(kk, i):
        hi, lo = split(jnp.concatenate([wv[kk, i, q] for q in range(SIDE)], axis=1))
        z_out[:, pl.ds(pl.multiple_of(i * 1024 + kk * 512, 512), 512)] = stack([hi, hi, lo])
        corner[0] = corner[0] + dot16(stack([hi[NB:], lo[NB:]]), stack([hi[:NB], lo[:NB]]), NT)

    for j in (0, 1, 3, 2):
        gathered(j)
        use(k, wrap(y + SIDE - j))
    for j in (0, 1, 3, 2):
        sibling_came(j)
        use(1 - k, wrap(y + SIDE - j))
    corner = corner[0][:NB] + corner[0][NB:]
    cbuf[x] = corner
    exchange(cbuf, CORNER)

    for d in range(1, SIDE):
        q = wrap(z + d)
        came(wv_rows.at[q], OWN_ROWS + q)
    pl.when(diagonal)(rows_local.wait)
    pl.when(jnp.logical_not(diagonal))(remote(wv_rows.at[z], wv_rows.at[z], OWN_ROWS, OWN_ROWS + z, sibling).wait_recv)
    own = jnp.concatenate([wv_rows[q] for q in range(SIDE)], axis=1)
    w_t, v_t = own[:NB], own[NB:]
    vt_out[...] = v_t
    finish()
    total = exchanged(cbuf, CORNER)
    w_t = w_t - dot(b_t, dot(total[:, :NB] + total[:, NB:], v_t))
    x_hi, x_lo = split(jnp.transpose(stack([v_t, w_t])))
    x_out[...] = jnp.concatenate([x_hi, x_lo, x_hi], axis=1)
    finish()


def update_kernel(a_ref, x_ref, z_ref, v_ref, out_ref, v_out):
    width = out_ref.shape[1]
    cols = pl.ds(pl.multiple_of(pl.program_id(0) * width, width), width)
    out_ref[...] = a_ref[:, cols] - dot16(x_ref[...], z_ref[:, cols])
    v_out[...] = v_ref[...]


def local(trailing):
    rows, cols = trailing.shape
    f32, b16 = jnp.float32, jnp.bfloat16
    vmem = pl.BlockSpec(memory_space=pltpu.VMEM)
    a_copy, x_mat, z_mat, v_t = pl.pallas_call(
        kernel,
        out_shape=(
            jax.ShapeDtypeStruct((rows, cols), f32),
            jax.ShapeDtypeStruct((rows, 6 * NB), b16),
            jax.ShapeDtypeStruct((6 * NB, cols), b16),
            jax.ShapeDtypeStruct((NB, rows), f32),
        ),
        in_specs=[pl.BlockSpec(memory_space=pl.ANY)],
        out_specs=(vmem, vmem, vmem, vmem),
        scratch_shapes=[
            pltpu.VMEM((2, SIDE, rows, 512), b16),
            pltpu.VMEM((2, SIDE, rows, 512), b16),
            pltpu.VMEM((rows, 128), f32),
            pltpu.VMEM((NB, cols), f32),
            pltpu.VMEM((SIDE, 128, 128), f32),
            pltpu.VMEM((NB, rows), f32),
            pltpu.VMEM((128, 128), f32),
            pltpu.VMEM((2, SIDE, SIDE, NB, 128), f32),
            pltpu.VMEM((SIDE, SIDE, NB, 128), f32),
            pltpu.VMEM((SIDE * SIDE, NB, 128), f32),
            pltpu.VMEM((2, SIDE, SIDE, 128, 128), f32),
            pltpu.VMEM((SIDE, 128, 128), f32),
            pltpu.VMEM((SIDE, NB, 128), f32),
            pltpu.VMEM((NB, 128), f32),
            pltpu.VMEM((SIDE, NB, 128), f32),
            pltpu.VMEM((128, 128), f32),
            pltpu.VMEM((NB, 128), f32),
            pltpu.SemaphoreType.DMA((9,)),
            pltpu.SemaphoreType.DMA((COUNT,)),
            pltpu.SemaphoreType.DMA((COUNT,)),
        ],
        compiler_params=pltpu.CompilerParams(
            collective_id=0, has_side_effects=True, vmem_limit_bytes=38 * 2**20
        ),
    )(trailing)
    step = 512
    reduced, v_t = pl.pallas_call(
        update_kernel,
        grid=(cols // step,),
        out_shape=(jax.ShapeDtypeStruct((rows, cols), f32), jax.ShapeDtypeStruct((NB, rows), f32)),
        in_specs=[vmem, vmem, vmem, vmem],
        out_specs=(pl.BlockSpec((rows, step), lambda i: (0, i)), pl.BlockSpec((NB, rows), lambda i: (0, 0))),
        compiler_params=pltpu.CompilerParams(vmem_limit_bytes=20 * 2**20),
    )(a_copy, x_mat, z_mat, v_t)
    return reduced, v_t.T


def solution(mesh):
    return jax.shard_map(
        local, mesh=mesh, in_specs=(P("row", "col"),), out_specs=(P("row", "col"), P("row", None)), check_vma=False
    )
```

```python
import jax
import jax.numpy as jnp
from jax import lax
from jax.experimental import pallas as pl
from jax.experimental.pallas import tpu as pltpu
from jax.sharding import PartitionSpec as P

NB = 64
BLOCK = 8
SIDE = 4
MESH = pl.DeviceIdType.MESH
HIGHEST = lax.Precision.HIGHEST
NN = (((1,), (0,)), ((), ()))
NT = (((1,), (1,)), ((), ()))
TN = (((0,), (0,)), ((), ()))


def dot(a, b, dims=NN):
    return lax.dot_general(a, b, dims, precision=HIGHEST, preferred_element_type=jnp.float32)


def dot16(a, b, dims=NN):
    return lax.dot_general(a, b, dims, preferred_element_type=jnp.float32)


def split(a):
    high = a.astype(jnp.bfloat16)
    return high, (a - high.astype(jnp.float32)).astype(jnp.bfloat16)


def split3(a):
    high = a.astype(jnp.bfloat16)
    rest = a - high.astype(jnp.float32)
    middle = rest.astype(jnp.bfloat16)
    return high, middle, (rest - middle.astype(jnp.float32)).astype(jnp.bfloat16)


def stack(parts):
    return jnp.concatenate(parts, axis=0)


def wrap(i):
    return i & (SIDE - 1)


def wrap_core(i):
    return i & 1


AROUND = [(2, 2), (2, 1), (2, 3), (1, 2), (3, 2), (1, 1), (3, 3), (1, 3), (3, 1), (2, 0), (0, 2), (1, 0), (3, 0), (0, 1), (0, 3)]


RING = (2, 1, 3, 0)


class Ids:
    def __init__(self):
        self.count = 0

    def take(self, n):
        first = self.count
        self.count += n
        return first


IDS = Ids()
ROWS = IDS.take(4)
HOME_P = IDS.take(32)
HOME_Q = IDS.take(4)
GRAM = IDS.take(8)
SPREAD = IDS.take(17)
HALVES = IDS.take(4)
SCATTER = IDS.take(16)
GATHER_P = IDS.take(10)
GATHER_W = IDS.take(20)
OWN_ROWS = IDS.take(4)
CORNER = IDS.take(8)
COUNT = IDS.count


def factor(gt, r_ref, c_ref, l_ref):
    lanes = lax.broadcasted_iota(jnp.int32, (8, 128), 1)
    subs = lax.broadcasted_iota(jnp.int32, (8, 128), 0)
    lane = lax.broadcasted_iota(jnp.int32, (1, 128), 1)
    t_all = jnp.transpose(stack([gt, jnp.zeros_like(gt)]))[NB:, :]
    S, T = [], []
    for b in range(8):
        rows = slice(8 * b, 8 * b + 8)
        unit = jnp.where(lanes == subs + (8 * b + NB), 1.0, 0.0)
        S.append(jnp.where(lanes < NB, gt[rows], unit))
        T.append(jnp.where(lanes < NB, t_all[rows], unit))

    def spread(row, j):
        return jnp.broadcast_to(row[:, j : j + 1], (1, 128))

    for j0 in range(0, NB, BLOCK):
        b, s0 = j0 // 8, j0 % 8
        srow = [S[b][s0 + p : s0 + p + 1, :] for p in range(BLOCK)]
        trow = [T[b][s0 + p : s0 + p + 1, :] for p in range(BLOCK)]
        s = [[spread(srow[p], j0 + q) if q >= p else None for q in range(BLOCK)] for p in range(BLOCK)]
        t = [[spread(trow[p], j0 + q) for q in range(BLOCK)] for p in range(BLOCK)]
        d_inv, root_inv, length, f = [], [], [], {}
        for p in range(BLOCK):
            d_inv.append(1.0 / s[p][p])
            root_inv.append(lax.rsqrt(s[p][p]))
            length.append(s[p][p] * root_inv[p])
            for i in range(p + 1, BLOCK):
                f[p, i] = s[p][i] * d_inv[p]
                for q in range(i, BLOCK):
                    s[i][q] = s[i][q] - f[p, i] * s[p][q]
                srow[i] = srow[i] - f[p, i] * srow[p]
        surow = [srow[p] * d_inv[p] for p in range(BLOCK)]
        turow, g = [], {}
        for p in range(BLOCK):
            j = j0 + p
            positive = t[p][p] >= 0.0
            pivot_inv = 1.0 / (jnp.abs(t[p][p]) + length[p])
            pivot_inv = jnp.where(positive, pivot_inv, -pivot_inv)
            lead_inv = jnp.where(positive, -root_inv[p], root_inv[p])
            rrow = jnp.where(lane >= j, srow[p] * lead_inv, 0.0)
            r_ref[NB + j : NB + j + 1, :] = rrow
            urow = jnp.where(lane < NB, trow[p] - rrow, trow[p])
            l_ref[j : j + 1, :] = trow[p]
            turow.append(urow * pivot_inv)
            later = jnp.where(lane == j, 1.0 - pivot_inv, turow[p])
            c_ref[j : j + 1, :] = jnp.where((lane >= j) & (lane < NB), later, 0.0)
            for q in range(p + 1, BLOCK):
                g[p, q] = (t[p][q] - s[p][q] * lead_inv) * pivot_inv
            for i in range(p + 1, BLOCK):
                for q in range(p + 1, BLOCK):
                    t[i][q] = t[i][q] - t[i][p] * g[p, q]
                trow[i] = trow[i] - t[i][p] * turow[p]
        for m in range((j0 + BLOCK) // 8, 8):
            sc, tc = [], []
            for p in range(BLOCK):
                sp, tp = S[m][:, j0 + p : j0 + p + 1], T[m][:, j0 + p : j0 + p + 1]
                sp, tp = jnp.broadcast_to(sp, (8, 128)), jnp.broadcast_to(tp, (8, 128))
                for i in range(p):
                    sp = sp - sc[i] * f[i, p]
                    tp = tp - tc[i] * g[i, p]
                sc.append(sp)
                tc.append(tp)
            for p in range(BLOCK):
                S[m] = S[m] - sc[p] * surow[p]
                T[m] = T[m] - tc[p] * turow[p]


def invert(c_ref):
    lanes = lax.broadcasted_iota(jnp.int32, (8, 128), 1)
    subs = lax.broadcasted_iota(jnp.int32, (8, 128), 0)
    C = [jnp.where(lanes == subs + 8 * b, 1.0, 0.0) for b in range(8)]
    for j0 in range(0, NB, BLOCK):
        rows = [c_ref[j0 + p : j0 + p + 1, :] for p in range(BLOCK)]
        g = {(i, p): jnp.broadcast_to(rows[i][:, j0 + p : j0 + p + 1], (1, 128)) for p in range(BLOCK) for i in range(p)}
        for m in range(j0 // 8 + 1):
            cols = []
            for p in range(BLOCK):
                col = jnp.broadcast_to(C[m][:, j0 + p : j0 + p + 1], (8, 128))
                for i in range(p):
                    col = col - cols[i] * g[i, p]
                cols.append(col)
            for p in range(BLOCK):
                C[m] = C[m] - cols[p] * rows[p]
    return stack(C)


def kernel(
    a_hbm, a_v, x_out, z_out, vt_out,
    a_hi, a_lo, head, lead, panel, prow, qpiece, dbuf, sbuf, rbuf, pbuf, wbuf, wrow, gbuf, gt_ref, cbuf, r_ref, c_ref, l_ref,
    load_sem, send, recv,
):
    r, x = lax.axis_index("row"), lax.axis_index("col")
    z, y, k = r // 8, lax.rem(r // 2, SIDE), lax.rem(r, 2)
    w = (1 - k) * z + k * y
    u = (1 - k) * y + k * z
    lanes64 = lax.broadcasted_iota(jnp.int32, (NB, 128), 1)

    def dev(z_, y_, k_, x_):
        return (z_ * 8 + y_ * 2 + k_, x_)

    def dev_w(d):
        return dev(wrap(z + d * (1 - k)), wrap(y + d * k), k, x)

    def dev_u(d):
        return dev(wrap(z + d * k), wrap(y + d * (1 - k)), k, x)

    def remote(src, dst, s, t, device):
        return pltpu.make_async_remote_copy(
            src_ref=src, dst_ref=dst, send_sem=send.at[s], recv_sem=recv.at[t],
            device_id=device, device_id_type=MESH,
        )

    sends = []

    def launch(copy, when=None):
        if when is None:
            copy.start()
        else:
            pl.when(when)(copy.start)
        sends.append((copy, when))

    def finish():
        for copy, when in sends:
            if when is None:
                copy.wait_send()
            else:
                pl.when(when)(copy.wait_send)
        sends.clear()

    sibling = dev(z, y, 1 - k, x)

    def came(dst, slot):
        remote(dst, dst, slot, slot, sibling).wait_recv()

    owns = x == 0
    first_row = r == 0
    first_chip = r < 2
    half = a_v.shape[0] // 2

    def head_load(q):
        rows = pl.ds(q * 128, 128)
        return pltpu.make_async_copy(a_hbm.at[rows, pl.ds(0, 128)], head.at[rows], load_sem.at[q])

    def load(i):
        rows = pl.ds(i * half, half)
        return pltpu.make_async_copy(a_hbm.at[rows], a_v.at[rows], load_sem.at[4 + i])

    lead_load = pltpu.make_async_copy(a_hbm.at[pl.ds(0, NB)], lead, load_sem.at[6])

    @pl.when(owns)
    def _():
        for q in range(SIDE):
            head_load(q).start()

    pl.when(first_row)(lead_load.start)
    barrier = pltpu.get_barrier_semaphore()
    peers = [dev(wrap(z + i), y, k, wrap(x + j)) for i in range(SIDE) for j in range(1, SIDE)]
    peers += [dev(wrap(z + i), wrap(y + j), k, x) for i, j in AROUND] + [sibling]
    peers += [dev(z, y, 1 - k, wrap(x + j)) for j in range(1, SIDE)]
    for peer in peers:
        pl.semaphore_signal(barrier, inc=1, device_id=peer, device_id_type=MESH)

    @pl.when((k == 1) & (r != 1))
    def _():
        pl.semaphore_signal(barrier, inc=1, device_id=dev(0, 0, 0, x), device_id_type=MESH)

    load(0).start()
    load(1).start()
    r_ref[0:NB, :] = jnp.zeros((NB, 128), jnp.float32)

    @pl.when(owns)
    def _():
        for q in range(SIDE):
            head_load(q).wait()
            panel[q] = jnp.transpose(head[q * 128 : (q + 1) * 128, :])
            if q == 0:
                panel[0, 0:NB] = jnp.where(first_row & (lanes64 < NB), 0.0, panel[0, 0:NB])
            prow[:, q * 128 : (q + 1) * 128] = panel[q, 0:NB]

    @pl.when(first_row)
    def _():
        lead_load.wait()
        lead[:, 0:128] = jnp.where(owns & (lanes64 < NB), 0.0, lead[:, 0:128])
        gram = jnp.zeros((3 * NB, 3 * NB), jnp.float32)
        for m in range(8):
            three = stack(split3(lead[:, m * 512 : (m + 1) * 512]))
            gram = gram + dot16(three, three, NT)
        gram = gram[:NB] + gram[NB : 2 * NB] + gram[2 * NB :]
        gram = gram[:, :NB] + gram[:, NB : 2 * NB] + gram[:, 2 * NB :]
        top = jnp.where(owns, lead[:, 0:128], 0.0)
        gbuf[x] = jnp.where(lanes64 < NB, jnp.concatenate([gram, gram], axis=1), top)

    def split_rows(part_id):
        load(part_id).wait()

        def body(step, carry):
            rows = pl.ds(pl.multiple_of(part_id * half + step * 16, 16), 16)
            for kk in range(2):
                for i in range(SIDE):
                    first = i * 1024 + kk * 512
                    a_hi[kk, i, rows, :], a_lo[kk, i, rows, :] = split(a_v[rows, first : first + 512])
            return carry

        lax.fori_loop(0, half // 16, body, 0)

    @pl.when(first_chip)
    def _():
        split_rows(0)
        split_rows(1)

    @pl.when(first_row)
    def _():
        pl.semaphore_wait(barrier, len(peers) + SIDE * SIDE - 1)

    @pl.when(jnp.logical_not(first_row))
    def _():
        pl.semaphore_wait(barrier, len(peers))


    for d in (2, 1, 3):
        launch(remote(prow, prow, ROWS + d, ROWS, dev(z, y, k, d)), owns)
    diagonal = x == z
    off_diagonal = jnp.logical_not(diagonal)

    def home_q(q):
        return remote(panel.at[q, pl.ds(NB, NB)], qpiece, HOME_Q + q, HOME_Q, dev(q, y, k, z))

    self_home = owns & (z == 0)
    home_local = pltpu.make_async_copy(panel.at[0, pl.ds(NB, NB)], qpiece, load_sem.at[7])

    def exchanged(buf, base):
        for d in range(1, SIDE):
            came(buf.at[wrap(x + SIDE - d)], base + d)
        return (buf[0] + buf[1]) + (buf[2] + buf[3])

    def own_piece():
        pbuf[0, 0, 0] = lead[:, 0:128]

    for d in (2, 1, 3):
        for kk in range(2):
            slot = GRAM + 2 * d + kk
            launch(remote(gbuf.at[x], gbuf.at[x], slot, GRAM + d, dev(0, 0, kk, wrap(x + d))), first_row)
    launch(remote(gbuf.at[x], gbuf.at[x], GRAM, GRAM, sibling), first_row)

    pl.when(first_row)(own_piece)
    for i, j in AROUND + [(0, 0)]:
        for kk in range(2):
            if i or j or kk:
                there = pbuf.at[kk, i if kk else j, j if kk else i]
                piece = lead.at[:, pl.ds(j * 1024 + kk * 512 + i * 128, 128)]
                launch(remote(piece, there, HOME_P + kk * 16 + i * SIDE + j, HOME_P, dev(i, j, kk, x)), first_row)

    @pl.when(jnp.logical_not(first_chip))
    def _():
        split_rows(0)
        split_rows(1)

    pl.when(r == 1)(remote(gbuf.at[x], gbuf.at[x], GRAM, GRAM, sibling).wait_recv)

    @pl.when(first_chip)
    def _():
        gt_ref[...] = exchanged(gbuf, GRAM)

    def gt_came():
        came(gt_ref, SPREAD)

    for i, j in AROUND:
        launch(remote(gt_ref, gt_ref, SPREAD + 4 * i + j, SPREAD, dev(wrap(z + i), wrap(y + j), k, x)), first_chip)

    pl.when(jnp.logical_not(owns))(remote(prow, prow, ROWS, ROWS, sibling).wait_recv)
    both = stack(split(prow[...]))

    def multiply(kk, i):
        new = dot16(both, a_hi[kk, i]) + dot16(both, a_lo[kk, i])
        return new[:NB] + new[NB:]

    for i in RING:
        j = wrap(y + i)
        new = multiply(1 - k, j)
        for q in range(SIDE):
            dbuf[1 - k, j, q] = new[:, q * 128 : (q + 1) * 128]
        launch(remote(dbuf.at[1 - k, j], sbuf.at[j], HALVES + i, HALVES + i, sibling))

    pl.when(jnp.logical_not(first_row))(remote(pbuf.at[k, u, w], pbuf.at[k, u, w], HOME_P, HOME_P, sibling).wait_recv)
    for d in (2, 1, 3):
        launch(remote(pbuf.at[k, u, w], pbuf.at[k, u, w], GATHER_P + d - 1, GATHER_P + d - 1, dev_w(d)))

    for i in RING:
        j = wrap(y + i)
        new = multiply(k, j)
        came(sbuf.at[j], HALVES + i)
        for q in range(SIDE):
            dbuf[k, j, q] = new[:, q * 128 : (q + 1) * 128] + sbuf[j, q]
        for h in RING:
            if h or i:
                q = wrap(z + h)
                slot = SCATTER + 4 * h + i
                launch(remote(dbuf.at[k, j, q], rbuf.at[4 * h + i], slot, slot, dev(q, j, k, x)))

    pl.when(self_home)(home_local.start)
    launch(home_q(0), owns & (z != 0))
    for q in range(1, SIDE):
        launch(home_q(q), owns)

    def sibling_send(buf, i, slot):
        launch(remote(buf.at[k, i], buf.at[k, i], slot, slot, sibling))

    for d in (1, 3, 2):
        came(pbuf.at[k, u, wrap(w + SIDE - d)], GATHER_P + d - 1)
    for d in (2, 1, 3):
        launch(remote(pbuf.at[k, u], pbuf.at[k, u], GATHER_P + 2 + d, GATHER_P + 2 + d, dev_u(d)))
    pl.when(jnp.logical_not(first_chip))(gt_came)
    factor(gt_ref[...], r_ref, c_ref, l_ref)
    r_all = r_ref[...]
    r_shift = jnp.transpose(r_all)[:NB, :]
    l_inv = l_ref[:, NB:]
    k_t = -dot(l_inv, r_all[NB:, NB:])

    pl.when(self_home)(home_local.wait)
    pl.when(jnp.logical_not(self_home))(remote(qpiece, qpiece, HOME_Q, HOME_Q, sibling).wait_recv)
    early = dot(l_inv, qpiece[...])
    total = dbuf[k, y, z]
    for slot in range(1, 16):
        came(rbuf.at[slot], SCATTER + slot)
        total = total + rbuf[slot]
    w_piece = early + dot(k_t, total)
    p_piece = pbuf[k, u, w] - jnp.where(first_row & owns, r_shift, 0.0)
    corner = dot(k_t, dot(p_piece, w_piece, NT))
    wbuf[k, y, z, 0:NB] = w_piece
    wbuf[k, y, z, NB:] = jnp.concatenate([corner[: NB // 2], corner[NB // 2 :]], axis=1)
    for i, j in AROUND:
        slot = GATHER_W + 4 * i + j
        launch(remote(wbuf.at[k, y, z], wbuf.at[k, y, z], slot, slot, dev(wrap(z + i), wrap(y + j), k, x)))
    rows_local = pltpu.make_async_copy(wbuf.at[k, y, z, pl.ds(0, NB)], wrow.at[z], load_sem.at[8])

    def rows_copy(d):
        return remote(wbuf.at[k, y, z, pl.ds(0, NB)], wrow.at[z], OWN_ROWS + d, OWN_ROWS + z, dev(x, y, k, wrap(x + d)))

    pl.when(diagonal)(rows_local.start)
    launch(rows_copy(0), off_diagonal)
    for d in (2, 1, 3):
        launch(rows_copy(d))

    m_all = invert(c_ref)
    mt = jnp.transpose(stack([m_all, jnp.zeros_like(m_all)]))[:NB, :NB]
    mt_hi, mt_lo = split(mt)
    shift = jnp.where(first_row, r_shift, 0.0)
    v_t = dot(mt, jnp.concatenate([prow[:, :128] - shift, prow[:, 128:]], axis=1))
    vt_out[...] = v_t
    shift = jnp.where(owns, r_shift, 0.0)

    def put(row, cols, hi, lo):
        z_out[row : row + NB, cols] = hi
        z_out[row + 2 * NB : row + 3 * NB, cols] = hi
        z_out[row + 4 * NB : row + 5 * NB, cols] = lo

    def make_v(kk, i):
        piece = jnp.concatenate([pbuf[kk, i, j] for j in range(SIDE)], axis=1)
        lead_shift = jnp.where((kk == 0) & (i == 0), shift, 0.0)
        hi, lo = split(jnp.concatenate([piece[:, :128] - lead_shift, piece[:, 128:]], axis=1))
        hi, lo = split((dot16(mt_lo, hi) + dot16(mt_hi, lo)) + dot16(mt_hi, hi))
        for j in range(SIDE):
            first = (1 - kk) * (i * 1024 + j * 128) + kk * (j * 1024 + 512 + i * 128)
            here = slice(j * 128, (j + 1) * 128)
            put(NB, pl.ds(pl.multiple_of(first, 128), 128), hi[:, here], lo[:, here])

    sibling_send(pbuf, u, GATHER_P + 6)
    for d in (1, 3, 2):
        came(pbuf.at[k, wrap(u + SIDE - d)], GATHER_P + 2 + d)
        sibling_send(pbuf, wrap(u + SIDE - d), GATHER_P + 6 + d)
    for d in range(SIDE):
        make_v(k, wrap(u + SIDE - d))
    for d in range(SIDE):
        came(pbuf.at[1 - k, wrap(w + SIDE - d)], GATHER_P + 6 + d)
        make_v(1 - k, wrap(w + SIDE - d))

    def use_w(kk, i):
        hi, lo = split(jnp.concatenate([wbuf[kk, i, q, 0:NB] for q in range(SIDE)], axis=1))
        put(0, pl.ds(pl.multiple_of(i * 1024 + kk * 512, 512), 512), hi, lo)

    corner = jnp.zeros((NB // 2, 128), jnp.float32)
    for j in (0, 1, 3, 2):
        for i in (0, 1, 3, 2):
            if i or j:
                came(wbuf.at[k, wrap(y + SIDE - j), wrap(z + SIDE - i)], GATHER_W + i * SIDE + j)
        sibling_send(wbuf, wrap(y + SIDE - j), GATHER_W + 16 + j)
    for i in range(SIDE):
        for q in range(SIDE):
            corner = corner + wbuf[k, i, q, NB:]
    cbuf[4 * k + x] = corner
    for d in (2, 1, 3):
        for kk in range(2):
            slot = CORNER + 2 * d + kk
            there = cbuf.at[4 * k + x]
            launch(remote(there, there, slot, slot, dev(z, y, wrap_core(k + kk), wrap(x + d))))
    launch(remote(cbuf.at[4 * k + x], cbuf.at[4 * k + x], CORNER + 1, CORNER + 1, sibling))

    for j in RING:
        use_w(k, wrap(y + SIDE - j))
    for j in (0, 1, 3, 2):
        came(wbuf.at[1 - k, wrap(y + SIDE - j)], GATHER_W + 16 + j)
        use_w(1 - k, wrap(y + SIDE - j))

    def own_came():
        for d in range(1, SIDE):
            q = wrap(z + d)
            came(wrow.at[q], OWN_ROWS + q)
        pl.when(diagonal)(rows_local.wait)
        pl.when(off_diagonal)(remote(wrow.at[z], wrow.at[z], OWN_ROWS, OWN_ROWS + z, sibling).wait_recv)

    own_came()
    w_t = jnp.concatenate([wrow[q] for q in range(SIDE)], axis=1)
    finish()
    came(cbuf.at[4 * wrap_core(k + 1) + x], CORNER + 1)
    for d in range(1, SIDE):
        for kk in range(2):
            came(cbuf.at[4 * wrap_core(k + kk) + wrap(x + SIDE - d)], CORNER + 2 * d + kk)
    corner = cbuf[0]
    for i in range(1, 2 * SIDE):
        corner = corner + cbuf[i]
    w_t = w_t - dot(stack([corner[:, :NB], corner[:, NB:]]), v_t)
    x_hi, x_lo = split(jnp.transpose(stack([v_t, w_t])))
    x_out[...] = jnp.concatenate([x_hi, x_lo, x_hi], axis=1)
    finish()


def update_kernel(a_ref, x_ref, z_ref, v_ref, out_hbm, v_hbm, buf, sem):
    parts, _, width = buf.shape
    v_copy = pltpu.make_async_copy(v_ref, v_hbm, sem.at[parts])
    v_copy.start()
    copies = []
    for i in range(parts):
        cols = slice(i * width, (i + 1) * width)
        buf[i] = a_ref[:, cols] - dot16(x_ref[...], z_ref[:, cols])
        copies.append(pltpu.make_async_copy(buf.at[i], out_hbm.at[:, pl.ds(i * width, width)], sem.at[i]))
        copies[i].start()
    for copy in copies:
        copy.wait()
    v_copy.wait()


def local(trailing):
    rows, cols = trailing.shape
    f32, b16 = jnp.float32, jnp.bfloat16
    vmem = pl.BlockSpec(memory_space=pltpu.VMEM)
    pieces = pltpu.VMEM((2, SIDE, SIDE, NB, 128), f32)
    square = pltpu.VMEM((SIDE, NB, 128), f32)
    a_copy, x_mat, z_mat, v_t = pl.pallas_call(
        kernel,
        out_shape=(
            jax.ShapeDtypeStruct((rows, cols), f32),
            jax.ShapeDtypeStruct((rows, 6 * NB), b16),
            jax.ShapeDtypeStruct((6 * NB, cols), b16),
            jax.ShapeDtypeStruct((NB, rows), f32),
        ),
        in_specs=[pl.BlockSpec(memory_space=pl.ANY)],
        out_specs=(vmem, vmem, vmem, vmem),
        scratch_shapes=[
            pltpu.VMEM((2, SIDE, rows, 512), b16),
            pltpu.VMEM((2, SIDE, rows, 512), b16),
            pltpu.VMEM((rows, 128), f32),
            pltpu.VMEM((NB, cols), f32),
            pltpu.VMEM((SIDE, 128, 128), f32),
            pltpu.VMEM((NB, rows), f32),
            pltpu.VMEM((NB, 128), f32),
            pieces,
            pltpu.VMEM((SIDE, SIDE, NB, 128), f32),
            pltpu.VMEM((SIDE * SIDE, NB, 128), f32),
            pieces,
            pltpu.VMEM((2, SIDE, SIDE, NB + NB // 2, 128), f32),
            square,
            square,
            pltpu.VMEM((NB, 128), f32),
            pltpu.VMEM((2 * SIDE, NB // 2, 128), f32),
            pltpu.VMEM((128, 128), f32),
            pltpu.VMEM((NB, 128), f32),
            pltpu.VMEM((NB, 128), f32),
            pltpu.SemaphoreType.DMA((9,)),
            pltpu.SemaphoreType.DMA((COUNT,)),
            pltpu.SemaphoreType.DMA((COUNT,)),
        ],
        compiler_params=pltpu.CompilerParams(
            collective_id=0, has_side_effects=True, vmem_limit_bytes=38 * 2**20
        ),
    )(trailing)
    step = 512
    hbm = pl.BlockSpec(memory_space=pl.ANY)
    reduced, v_t = pl.pallas_call(
        update_kernel,
        out_shape=(jax.ShapeDtypeStruct((rows, cols), f32), jax.ShapeDtypeStruct((NB, rows), f32)),
        in_specs=[vmem, vmem, vmem, vmem],
        out_specs=(hbm, hbm),
        scratch_shapes=[pltpu.VMEM((cols // step, rows, step), f32), pltpu.SemaphoreType.DMA((cols // step + 1,))],
        compiler_params=pltpu.CompilerParams(vmem_limit_bytes=24 * 2**20),
    )(a_copy, x_mat, z_mat, v_t)
    return reduced, v_t.T


def solution(mesh):
    return jax.shard_map(
        local, mesh=mesh, in_specs=(P("row", "col"),), out_specs=(P("row", "col"), P("row", None)), check_vma=False
    )
```

```python
import jax
import jax.numpy as jnp
from jax import lax
from jax.experimental import pallas as pl
from jax.experimental.pallas import tpu as pltpu
from jax.sharding import PartitionSpec as P

NB = 64
BLOCK = 8
SIDE = 4
MESH = pl.DeviceIdType.MESH
HIGHEST = lax.Precision.HIGHEST
NN = (((1,), (0,)), ((), ()))
NT = (((1,), (1,)), ((), ()))
TN = (((0,), (0,)), ((), ()))


def dot(a, b, dims=NN):
    return lax.dot_general(a, b, dims, precision=HIGHEST, preferred_element_type=jnp.float32)


def dot16(a, b, dims=NN):
    return lax.dot_general(a, b, dims, preferred_element_type=jnp.float32)


def split(a):
    high = a.astype(jnp.bfloat16)
    return high, (a - high.astype(jnp.float32)).astype(jnp.bfloat16)


def split3(a):
    high = a.astype(jnp.bfloat16)
    rest = a - high.astype(jnp.float32)
    middle = rest.astype(jnp.bfloat16)
    return high, middle, (rest - middle.astype(jnp.float32)).astype(jnp.bfloat16)


def stack(parts):
    return jnp.concatenate(parts, axis=0)


def wrap(i):
    return i & (SIDE - 1)


def wrap_core(i):
    return i & 1


AROUND = [(2, 2), (2, 1), (2, 3), (1, 2), (3, 2), (1, 1), (3, 3), (1, 3), (3, 1), (2, 0), (0, 2), (1, 0), (3, 0), (0, 1), (0, 3)]


RING = (2, 1, 3, 0)


class Ids:
    def __init__(self):
        self.count = 0

    def take(self, n):
        first = self.count
        self.count += n
        return first


IDS = Ids()
ROWS = IDS.take(4)
HOME_P = IDS.take(32)
HOME_Q = IDS.take(4)
GRAM = IDS.take(8)
SPREAD = IDS.take(17)
HALVES = IDS.take(4)
SCATTER = IDS.take(16)
GATHER_P = IDS.take(10)
GATHER_W = IDS.take(20)
OWN_ROWS = IDS.take(4)
CORNER = IDS.take(8)
CORNER_P = IDS.take(16)
COUNT = IDS.count


def factor(gt, r_ref, c_ref, l_ref):
    lanes = lax.broadcasted_iota(jnp.int32, (8, 128), 1)
    subs = lax.broadcasted_iota(jnp.int32, (8, 128), 0)
    lane = lax.broadcasted_iota(jnp.int32, (1, 128), 1)
    t_all = jnp.transpose(stack([gt, jnp.zeros_like(gt)]))[NB:, :]
    S, T = [], []
    for b in range(8):
        rows = slice(8 * b, 8 * b + 8)
        unit = jnp.where(lanes == subs + (8 * b + NB), 1.0, 0.0)
        S.append(jnp.where(lanes < NB, gt[rows], unit))
        T.append(jnp.where(lanes < NB, t_all[rows], unit))

    def spread(row, j):
        return jnp.broadcast_to(row[:, j : j + 1], (1, 128))

    for j0 in range(0, NB, BLOCK):
        b, s0 = j0 // 8, j0 % 8
        srow = [S[b][s0 + p : s0 + p + 1, :] for p in range(BLOCK)]
        trow = [T[b][s0 + p : s0 + p + 1, :] for p in range(BLOCK)]
        s = [[spread(srow[p], j0 + q) if q >= p else None for q in range(BLOCK)] for p in range(BLOCK)]
        t = [[spread(trow[p], j0 + q) for q in range(BLOCK)] for p in range(BLOCK)]
        d_inv, root_inv, length, f = [], [], [], {}
        for p in range(BLOCK):
            d_inv.append(1.0 / s[p][p])
            root_inv.append(lax.rsqrt(s[p][p]))
            length.append(s[p][p] * root_inv[p])
            for i in range(p + 1, BLOCK):
                f[p, i] = s[p][i] * d_inv[p]
                for q in range(i, BLOCK):
                    s[i][q] = s[i][q] - f[p, i] * s[p][q]
                srow[i] = srow[i] - f[p, i] * srow[p]
        surow = [srow[p] * d_inv[p] for p in range(BLOCK)]
        turow, g = [], {}
        for p in range(BLOCK):
            j = j0 + p
            positive = t[p][p] >= 0.0
            pivot_inv = 1.0 / (jnp.abs(t[p][p]) + length[p])
            pivot_inv = jnp.where(positive, pivot_inv, -pivot_inv)
            lead_inv = jnp.where(positive, -root_inv[p], root_inv[p])
            rrow = jnp.where(lane >= j, srow[p] * lead_inv, 0.0)
            r_ref[NB + j : NB + j + 1, :] = rrow
            urow = jnp.where(lane < NB, trow[p] - rrow, trow[p])
            l_ref[j : j + 1, :] = trow[p]
            turow.append(urow * pivot_inv)
            later = jnp.where(lane == j, 1.0 - pivot_inv, turow[p])
            c_ref[j : j + 1, :] = jnp.where((lane >= j) & (lane < NB), later, 0.0)
            for q in range(p + 1, BLOCK):
                g[p, q] = (t[p][q] - s[p][q] * lead_inv) * pivot_inv
            for i in range(p + 1, BLOCK):
                for q in range(p + 1, BLOCK):
                    t[i][q] = t[i][q] - t[i][p] * g[p, q]
                trow[i] = trow[i] - t[i][p] * turow[p]
        for m in range((j0 + BLOCK) // 8, 8):
            sc, tc = [], []
            for p in range(BLOCK):
                sp, tp = S[m][:, j0 + p : j0 + p + 1], T[m][:, j0 + p : j0 + p + 1]
                sp, tp = jnp.broadcast_to(sp, (8, 128)), jnp.broadcast_to(tp, (8, 128))
                for i in range(p):
                    sp = sp - sc[i] * f[i, p]
                    tp = tp - tc[i] * g[i, p]
                sc.append(sp)
                tc.append(tp)
            for p in range(BLOCK):
                S[m] = S[m] - sc[p] * surow[p]
                T[m] = T[m] - tc[p] * turow[p]


def invert(c_ref):
    lanes = lax.broadcasted_iota(jnp.int32, (8, 128), 1)
    subs = lax.broadcasted_iota(jnp.int32, (8, 128), 0)
    C = [jnp.where(lanes == subs + 8 * b, 1.0, 0.0) for b in range(8)]
    for j0 in range(0, NB, BLOCK):
        rows = [c_ref[j0 + p : j0 + p + 1, :] for p in range(BLOCK)]
        g = {(i, p): jnp.broadcast_to(rows[i][:, j0 + p : j0 + p + 1], (1, 128)) for p in range(BLOCK) for i in range(p)}
        for m in range(j0 // 8 + 1):
            cols = []
            for p in range(BLOCK):
                col = jnp.broadcast_to(C[m][:, j0 + p : j0 + p + 1], (8, 128))
                for i in range(p):
                    col = col - cols[i] * g[i, p]
                cols.append(col)
            for p in range(BLOCK):
                C[m] = C[m] - cols[p] * rows[p]
    return stack(C)


def kernel(
    a_hbm, a_v, x_out, z_out, vt_out,
    a_hi, a_lo, head, lead, panel, prow, qpiece, dbuf, sbuf, rbuf, pbuf, wbuf, wrow, gbuf, gt_ref, cbuf, r_ref, c_ref, l_ref,
    load_sem, send, recv,
):
    r, x = lax.axis_index("row"), lax.axis_index("col")
    z, y, k = r // 8, lax.rem(r // 2, SIDE), lax.rem(r, 2)
    w = (1 - k) * z + k * y
    u = (1 - k) * y + k * z
    lanes64 = lax.broadcasted_iota(jnp.int32, (NB, 128), 1)

    def dev(z_, y_, k_, x_):
        return (z_ * 8 + y_ * 2 + k_, x_)

    def dev_w(d):
        return dev(wrap(z + d * (1 - k)), wrap(y + d * k), k, x)

    def dev_u(d):
        return dev(wrap(z + d * k), wrap(y + d * (1 - k)), k, x)

    def remote(src, dst, s, t, device):
        return pltpu.make_async_remote_copy(
            src_ref=src, dst_ref=dst, send_sem=send.at[s], recv_sem=recv.at[t],
            device_id=device, device_id_type=MESH,
        )

    sends = []

    def launch(copy, when=None):
        if when is None:
            copy.start()
        else:
            pl.when(when)(copy.start)
        sends.append((copy, when))

    def finish():
        for copy, when in sends:
            if when is None:
                copy.wait_send()
            else:
                pl.when(when)(copy.wait_send)
        sends.clear()

    sibling = dev(z, y, 1 - k, x)

    def came(dst, slot):
        remote(dst, dst, slot, slot, sibling).wait_recv()

    owns = x == 0
    first_row = r == 0
    first_chip = r < 2
    half = a_v.shape[0] // 2

    def head_load(q):
        rows = pl.ds(q * 128, 128)
        return pltpu.make_async_copy(a_hbm.at[rows, pl.ds(0, 128)], head.at[rows], load_sem.at[q])

    def load(i):
        rows = pl.ds(i * half, half)
        return pltpu.make_async_copy(a_hbm.at[rows], a_v.at[rows], load_sem.at[4 + i])

    lead_load = pltpu.make_async_copy(a_hbm.at[pl.ds(0, NB)], lead, load_sem.at[6])

    @pl.when(owns)
    def _():
        for q in range(SIDE):
            head_load(q).start()

    pl.when(first_row)(lead_load.start)
    barrier = pltpu.get_barrier_semaphore()
    peers = [dev(wrap(z + i), y, k, wrap(x + j)) for i in range(SIDE) for j in range(1, SIDE)]
    peers += [dev(wrap(z + i), wrap(y + j), k, x) for i, j in AROUND] + [sibling]
    peers += [dev(z, y, 1 - k, wrap(x + j)) for j in range(1, SIDE)]
    for peer in peers:
        pl.semaphore_signal(barrier, inc=1, device_id=peer, device_id_type=MESH)

    @pl.when((k == 1) & (r != 1))
    def _():
        pl.semaphore_signal(barrier, inc=1, device_id=dev(0, 0, 0, x), device_id_type=MESH)

    load(0).start()
    load(1).start()
    r_ref[0:NB, :] = jnp.zeros((NB, 128), jnp.float32)

    @pl.when(owns)
    def _():
        for q in range(SIDE):
            head_load(q).wait()
            panel[q] = jnp.transpose(head[q * 128 : (q + 1) * 128, :])
            if q == 0:
                panel[0, 0:NB] = jnp.where(first_row & (lanes64 < NB), 0.0, panel[0, 0:NB])
            prow[:, q * 128 : (q + 1) * 128] = panel[q, 0:NB]

    @pl.when(first_row)
    def _():
        lead_load.wait()
        lead[:, 0:128] = jnp.where(owns & (lanes64 < NB), 0.0, lead[:, 0:128])
        gram = jnp.zeros((3 * NB, 3 * NB), jnp.float32)
        for m in range(8):
            three = stack(split3(lead[:, m * 512 : (m + 1) * 512]))
            gram = gram + dot16(three, three, NT)
        gram = gram[:NB] + gram[NB : 2 * NB] + gram[2 * NB :]
        gram = gram[:, :NB] + gram[:, NB : 2 * NB] + gram[:, 2 * NB :]
        top = jnp.where(owns, lead[:, 0:128], 0.0)
        gbuf[x] = jnp.where(lanes64 < NB, jnp.concatenate([gram, gram], axis=1), top)

    def split_rows(part_id):
        load(part_id).wait()

        def body(step, carry):
            rows = pl.ds(pl.multiple_of(part_id * half + step * 16, 16), 16)
            for kk in range(2):
                for i in range(SIDE):
                    first = i * 1024 + kk * 512
                    a_hi[kk, i, rows, :], a_lo[kk, i, rows, :] = split(a_v[rows, first : first + 512])
            return carry

        lax.fori_loop(0, half // 16, body, 0)

    @pl.when(first_chip)
    def _():
        split_rows(0)
        split_rows(1)

    @pl.when(first_row)
    def _():
        pl.semaphore_wait(barrier, len(peers) + SIDE * SIDE - 1)

    @pl.when(jnp.logical_not(first_row))
    def _():
        pl.semaphore_wait(barrier, len(peers))


    for d in (2, 1, 3):
        launch(remote(prow, prow, ROWS + d, ROWS, dev(z, y, k, d)), owns)
    diagonal = x == z
    off_diagonal = jnp.logical_not(diagonal)

    def home_q(q):
        return remote(panel.at[q, pl.ds(NB, NB)], qpiece, HOME_Q + q, HOME_Q, dev(q, y, k, z))

    self_home = owns & (z == 0)
    home_local = pltpu.make_async_copy(panel.at[0, pl.ds(NB, NB)], qpiece, load_sem.at[7])

    def exchanged(buf, base):
        for d in range(1, SIDE):
            came(buf.at[wrap(x + SIDE - d)], base + d)
        return (buf[0] + buf[1]) + (buf[2] + buf[3])

    def own_piece():
        pbuf[0, 0, 0] = lead[:, 0:128]

    for d in (2, 1, 3):
        for kk in range(2):
            slot = GRAM + 2 * d + kk
            launch(remote(gbuf.at[x], gbuf.at[x], slot, GRAM + d, dev(0, 0, kk, wrap(x + d))), first_row)
    launch(remote(gbuf.at[x], gbuf.at[x], GRAM, GRAM, sibling), first_row)

    pl.when(first_row)(own_piece)
    for i, j in AROUND + [(0, 0)]:
        for kk in range(2):
            if i or j or kk:
                there = pbuf.at[kk, i if kk else j, j if kk else i]
                piece = lead.at[:, pl.ds(j * 1024 + kk * 512 + i * 128, 128)]
                launch(remote(piece, there, HOME_P + kk * 16 + i * SIDE + j, HOME_P, dev(i, j, kk, x)), first_row)

    @pl.when(jnp.logical_not(first_chip))
    def _():
        split_rows(0)
        split_rows(1)

    pl.when(r == 1)(remote(gbuf.at[x], gbuf.at[x], GRAM, GRAM, sibling).wait_recv)

    @pl.when(first_chip)
    def _():
        gt_ref[...] = exchanged(gbuf, GRAM)

    def gt_came():
        came(gt_ref, SPREAD)

    for i, j in AROUND:
        launch(remote(gt_ref, gt_ref, SPREAD + 4 * i + j, SPREAD, dev(wrap(z + i), wrap(y + j), k, x)), first_chip)

    pl.when(jnp.logical_not(owns))(remote(prow, prow, ROWS, ROWS, sibling).wait_recv)
    both = stack(split(prow[...]))

    def multiply(kk, i):
        new = dot16(both, a_hi[kk, i]) + dot16(both, a_lo[kk, i])
        return new[:NB] + new[NB:]

    for i in RING:
        j = wrap(y + i)
        new = multiply(1 - k, j)
        for q in range(SIDE):
            dbuf[1 - k, j, q] = new[:, q * 128 : (q + 1) * 128]
        launch(remote(dbuf.at[1 - k, j], sbuf.at[j], HALVES + i, HALVES + i, sibling))

    pl.when(jnp.logical_not(first_row))(remote(pbuf.at[k, u, w], pbuf.at[k, u, w], HOME_P, HOME_P, sibling).wait_recv)
    for d in (2, 1, 3):
        launch(remote(pbuf.at[k, u, w], pbuf.at[k, u, w], GATHER_P + d - 1, GATHER_P + d - 1, dev_w(d)))

    for i in RING:
        j = wrap(y + i)
        new = multiply(k, j)
        came(sbuf.at[j], HALVES + i)
        for q in range(SIDE):
            dbuf[k, j, q] = new[:, q * 128 : (q + 1) * 128] + sbuf[j, q]
        for h in RING:
            if h or i:
                q = wrap(z + h)
                slot = SCATTER + 4 * h + i
                launch(remote(dbuf.at[k, j, q], rbuf.at[4 * h + i], slot, slot, dev(q, j, k, x)))

    pl.when(self_home)(home_local.start)
    launch(home_q(0), owns & (z != 0))
    for q in range(1, SIDE):
        launch(home_q(q), owns)

    def sibling_send(buf, i, slot):
        launch(remote(buf.at[k, i], buf.at[k, i], slot, slot, sibling))

    for d in (1, 3, 2):
        came(pbuf.at[k, u, wrap(w + SIDE - d)], GATHER_P + d - 1)
    for d in (2, 1, 3):
        launch(remote(pbuf.at[k, u], pbuf.at[k, u], GATHER_P + 2 + d, GATHER_P + 2 + d, dev_u(d)))
    pl.when(jnp.logical_not(first_chip))(gt_came)
    factor(gt_ref[...], r_ref, c_ref, l_ref)
    r_all = r_ref[...]
    r_shift = jnp.transpose(r_all)[:NB, :]
    l_inv = l_ref[:, NB:]
    k_t = -dot(l_inv, r_all[NB:, NB:])

    pl.when(self_home)(home_local.wait)
    pl.when(jnp.logical_not(self_home))(remote(qpiece, qpiece, HOME_Q, HOME_Q, sibling).wait_recv)
    early = dot(l_inv, qpiece[...])
    k_p = dot(k_t, pbuf[k, u, w] - jnp.where(first_row & owns, r_shift, 0.0))
    total = dbuf[k, y, z]
    for slot in range(1, 16):
        came(rbuf.at[slot], SCATTER + slot)
        total = total + rbuf[slot]
    wbuf[k, y, z] = early + dot(k_t, total)
    corner = dot(k_p, wbuf[k, y, z], NT)
    mine = 4 * k + x
    cbuf[mine] = jnp.concatenate([corner[: NB // 2], corner[NB // 2 :]], axis=1)
    for d in (2, 1, 3):
        for kk in range(2):
            slot = CORNER + 2 * d + kk
            launch(remote(cbuf.at[mine], cbuf.at[mine], slot, slot, dev(z, y, wrap_core(k + kk), wrap(x + d))))
    launch(remote(cbuf.at[mine], cbuf.at[mine], CORNER + 1, CORNER + 1, sibling))

    for i, j in AROUND:
        slot = GATHER_W + 4 * i + j
        launch(remote(wbuf.at[k, y, z], wbuf.at[k, y, z], slot, slot, dev(wrap(z + i), wrap(y + j), k, x)))

    rows_local = pltpu.make_async_copy(wbuf.at[k, y, z], wrow.at[z], load_sem.at[8])

    def rows_copy(d):
        return remote(wbuf.at[k, y, z], wrow.at[z], OWN_ROWS + d, OWN_ROWS + z, dev(x, y, k, wrap(x + d)))

    pl.when(diagonal)(rows_local.start)
    launch(rows_copy(0), off_diagonal)
    for d in (2, 1, 3):
        launch(rows_copy(d))

    m_all = invert(c_ref)

    came(cbuf.at[4 * wrap_core(k + 1) + x], CORNER + 1)
    for d in range(1, SIDE):
        for kk in range(2):
            came(cbuf.at[4 * wrap_core(k + kk) + wrap(x + SIDE - d)], CORNER + 2 * d + kk)
    corner = cbuf[0]
    for i in range(1, 8):
        corner = corner + cbuf[i]
    cbuf[8] = corner
    for i, j in AROUND:
        slot = 4 * i + j
        launch(remote(cbuf.at[8], cbuf.at[8 + slot], CORNER_P + slot, CORNER_P + slot, dev(wrap(z + i), wrap(y + j), k, x)))

    mt = jnp.transpose(stack([m_all, jnp.zeros_like(m_all)]))[:NB, :NB]
    mt_hi, mt_lo = split(mt)
    shift = jnp.where(first_row, r_shift, 0.0)
    v_t = dot(mt, jnp.concatenate([prow[:, :128] - shift, prow[:, 128:]], axis=1))
    vt_out[...] = v_t
    shift = jnp.where(owns, r_shift, 0.0)

    def put(row, cols, hi, lo):
        z_out[row : row + NB, cols] = hi
        z_out[row + 2 * NB : row + 3 * NB, cols] = hi
        z_out[row + 4 * NB : row + 5 * NB, cols] = lo

    def make_v(kk, i):
        piece = jnp.concatenate([pbuf[kk, i, j] for j in range(SIDE)], axis=1)
        lead_shift = jnp.where((kk == 0) & (i == 0), shift, 0.0)
        hi, lo = split(jnp.concatenate([piece[:, :128] - lead_shift, piece[:, 128:]], axis=1))
        hi, lo = split((dot16(mt_lo, hi) + dot16(mt_hi, lo)) + dot16(mt_hi, hi))
        for j in range(SIDE):
            first = (1 - kk) * (i * 1024 + j * 128) + kk * (j * 1024 + 512 + i * 128)
            here = slice(j * 128, (j + 1) * 128)
            put(NB, pl.ds(pl.multiple_of(first, 128), 128), hi[:, here], lo[:, here])

    sibling_send(pbuf, u, GATHER_P + 6)
    for d in (1, 3, 2):
        came(pbuf.at[k, wrap(u + SIDE - d)], GATHER_P + 2 + d)
        sibling_send(pbuf, wrap(u + SIDE - d), GATHER_P + 6 + d)
    for d in range(SIDE):
        make_v(k, wrap(u + SIDE - d))
    for d in range(SIDE):
        came(pbuf.at[1 - k, wrap(w + SIDE - d)], GATHER_P + 6 + d)
        make_v(1 - k, wrap(w + SIDE - d))

    def use_w(kk, i):
        hi, lo = split(jnp.concatenate([wbuf[kk, i, q] for q in range(SIDE)], axis=1))
        put(0, pl.ds(pl.multiple_of(i * 1024 + kk * 512, 512), 512), hi, lo)

    for j in (0, 1, 3, 2):
        for i in (0, 1, 3, 2):
            if i or j:
                came(wbuf.at[k, wrap(y + SIDE - j), wrap(z + SIDE - i)], GATHER_W + i * SIDE + j)
        sibling_send(wbuf, wrap(y + SIDE - j), GATHER_W + 16 + j)
    for j in RING:
        use_w(k, wrap(y + SIDE - j))
    for j in (0, 1, 3, 2):
        came(wbuf.at[1 - k, wrap(y + SIDE - j)], GATHER_W + 16 + j)
        use_w(1 - k, wrap(y + SIDE - j))

    def own_came():
        for d in range(1, SIDE):
            q = wrap(z + d)
            came(wrow.at[q], OWN_ROWS + q)
        pl.when(diagonal)(rows_local.wait)
        pl.when(off_diagonal)(remote(wrow.at[z], wrow.at[z], OWN_ROWS, OWN_ROWS + z, sibling).wait_recv)

    own_came()
    w_t = jnp.concatenate([wrow[q] for q in range(SIDE)], axis=1)
    finish()
    corner = cbuf[8]
    for slot in range(1, 16):
        came(cbuf.at[8 + slot], CORNER_P + slot)
        corner = corner + cbuf[8 + slot]
    w_t = w_t - dot(stack([corner[:, :NB], corner[:, NB:]]), v_t)
    x_hi, x_lo = split(jnp.transpose(stack([v_t, w_t])))
    x_out[...] = jnp.concatenate([x_hi, x_lo, x_hi], axis=1)
    finish()


def update_kernel(a_ref, x_ref, z_ref, v_ref, out_hbm, v_hbm, buf, sem):
    parts, _, width = buf.shape
    v_copy = pltpu.make_async_copy(v_ref, v_hbm, sem.at[parts])
    v_copy.start()
    copies = []
    for i in range(parts):
        cols = slice(i * width, (i + 1) * width)
        buf[i] = a_ref[:, cols] - dot16(x_ref[...], z_ref[:, cols])
        copies.append(pltpu.make_async_copy(buf.at[i], out_hbm.at[:, pl.ds(i * width, width)], sem.at[i]))
        copies[i].start()
    for copy in copies:
        copy.wait()
    v_copy.wait()


def local(trailing):
    rows, cols = trailing.shape
    f32, b16 = jnp.float32, jnp.bfloat16
    vmem = pl.BlockSpec(memory_space=pltpu.VMEM)
    pieces = pltpu.VMEM((2, SIDE, SIDE, NB, 128), f32)
    square = pltpu.VMEM((SIDE, NB, 128), f32)
    a_copy, x_mat, z_mat, v_t = pl.pallas_call(
        kernel,
        out_shape=(
            jax.ShapeDtypeStruct((rows, cols), f32),
            jax.ShapeDtypeStruct((rows, 6 * NB), b16),
            jax.ShapeDtypeStruct((6 * NB, cols), b16),
            jax.ShapeDtypeStruct((NB, rows), f32),
        ),
        in_specs=[pl.BlockSpec(memory_space=pl.ANY)],
        out_specs=(vmem, vmem, vmem, vmem),
        scratch_shapes=[
            pltpu.VMEM((2, SIDE, rows, 512), b16),
            pltpu.VMEM((2, SIDE, rows, 512), b16),
            pltpu.VMEM((rows, 128), f32),
            pltpu.VMEM((NB, cols), f32),
            pltpu.VMEM((SIDE, 128, 128), f32),
            pltpu.VMEM((NB, rows), f32),
            pltpu.VMEM((NB, 128), f32),
            pieces,
            pltpu.VMEM((SIDE, SIDE, NB, 128), f32),
            pltpu.VMEM((SIDE * SIDE, NB, 128), f32),
            pieces,
            pieces,
            square,
            square,
            pltpu.VMEM((NB, 128), f32),
            pltpu.VMEM((6 * SIDE, NB // 2, 128), f32),
            pltpu.VMEM((128, 128), f32),
            pltpu.VMEM((NB, 128), f32),
            pltpu.VMEM((NB, 128), f32),
            pltpu.SemaphoreType.DMA((9,)),
            pltpu.SemaphoreType.DMA((COUNT,)),
            pltpu.SemaphoreType.DMA((COUNT,)),
        ],
        compiler_params=pltpu.CompilerParams(
            collective_id=0, has_side_effects=True, vmem_limit_bytes=38 * 2**20
        ),
    )(trailing)
    step = 512
    hbm = pl.BlockSpec(memory_space=pl.ANY)
    reduced, v_t = pl.pallas_call(
        update_kernel,
        out_shape=(jax.ShapeDtypeStruct((rows, cols), f32), jax.ShapeDtypeStruct((NB, rows), f32)),
        in_specs=[vmem, vmem, vmem, vmem],
        out_specs=(hbm, hbm),
        scratch_shapes=[pltpu.VMEM((cols // step, rows, step), f32), pltpu.SemaphoreType.DMA((cols // step + 1,))],
        compiler_params=pltpu.CompilerParams(vmem_limit_bytes=24 * 2**20),
    )(a_copy, x_mat, z_mat, v_t)
    return reduced, v_t.T


def solution(mesh):
    return jax.shard_map(
        local, mesh=mesh, in_specs=(P("row", "col"),), out_specs=(P("row", "col"), P("row", None)), check_vma=False
    )
```

```python
import jax
import jax.numpy as jnp
from jax import lax
from jax.experimental import pallas as pl
from jax.experimental.pallas import tpu as pltpu
from jax.sharding import PartitionSpec as P

NB = 64
BLOCK = 8
SIDE = 4
MESH = pl.DeviceIdType.MESH
HIGHEST = lax.Precision.HIGHEST
NN = (((1,), (0,)), ((), ()))
NT = (((1,), (1,)), ((), ()))
TN = (((0,), (0,)), ((), ()))


def dot(a, b, dims=NN):
    return lax.dot_general(a, b, dims, precision=HIGHEST, preferred_element_type=jnp.float32)


def dot16(a, b, dims=NN):
    return lax.dot_general(a, b, dims, preferred_element_type=jnp.float32)


def split(a):
    high = a.astype(jnp.bfloat16)
    return high, (a - high.astype(jnp.float32)).astype(jnp.bfloat16)


def split3(a):
    high = a.astype(jnp.bfloat16)
    rest = a - high.astype(jnp.float32)
    middle = rest.astype(jnp.bfloat16)
    return high, middle, (rest - middle.astype(jnp.float32)).astype(jnp.bfloat16)


def stack(parts):
    return jnp.concatenate(parts, axis=0)


def wrap(i):
    return i & (SIDE - 1)


def wrap_core(i):
    return i & 1


AROUND = [(2, 2), (2, 1), (2, 3), (1, 2), (3, 2), (1, 1), (3, 3), (1, 3), (3, 1), (2, 0), (0, 2), (1, 0), (3, 0), (0, 1), (0, 3)]


RING = (2, 1, 3, 0)


class Ids:
    def __init__(self):
        self.count = 0

    def take(self, n):
        first = self.count
        self.count += n
        return first


IDS = Ids()
ROWS = IDS.take(4)
HOME_P = IDS.take(32)
HOME_Q = IDS.take(4)
GRAM = IDS.take(8)
SPREAD = IDS.take(17)
HALVES = IDS.take(4)
SCATTER = IDS.take(16)
GATHER_P = IDS.take(10)
GATHER_W = IDS.take(20)
OWN_ROWS = IDS.take(4)
CORNER = IDS.take(8)
CORNER_P = IDS.take(16)
COUNT = IDS.count


def factor(gt, r_ref, c_ref, l_ref):
    lanes = lax.broadcasted_iota(jnp.int32, (8, 128), 1)
    subs = lax.broadcasted_iota(jnp.int32, (8, 128), 0)
    lane = lax.broadcasted_iota(jnp.int32, (1, 128), 1)
    t_all = jnp.transpose(stack([gt, jnp.zeros_like(gt)]))[NB:, :]
    S, T = [], []
    for b in range(8):
        rows = slice(8 * b, 8 * b + 8)
        unit = jnp.where(lanes == subs + (8 * b + NB), 1.0, 0.0)
        S.append(jnp.where(lanes < NB, gt[rows], unit))
        T.append(jnp.where(lanes < NB, t_all[rows], unit))

    def spread(row, j):
        return jnp.broadcast_to(row[:, j : j + 1], (1, 128))

    for j0 in range(0, NB, BLOCK):
        b, s0 = j0 // 8, j0 % 8
        srow = [S[b][s0 + p : s0 + p + 1, :] for p in range(BLOCK)]
        trow = [T[b][s0 + p : s0 + p + 1, :] for p in range(BLOCK)]
        s = [[spread(srow[p], j0 + q) if q >= p else None for q in range(BLOCK)] for p in range(BLOCK)]
        t = [[spread(trow[p], j0 + q) for q in range(BLOCK)] for p in range(BLOCK)]
        d_inv, root_inv, length, f = [], [], [], {}
        for p in range(BLOCK):
            d_inv.append(1.0 / s[p][p])
            root_inv.append(lax.rsqrt(s[p][p]))
            length.append(s[p][p] * root_inv[p])
            for i in range(p + 1, BLOCK):
                f[p, i] = s[p][i] * d_inv[p]
                for q in range(i, BLOCK):
                    s[i][q] = s[i][q] - f[p, i] * s[p][q]
                srow[i] = srow[i] - f[p, i] * srow[p]
        surow = [srow[p] * d_inv[p] for p in range(BLOCK)]
        turow, g = [], {}
        for p in range(BLOCK):
            j = j0 + p
            positive = t[p][p] >= 0.0
            pivot_inv = 1.0 / (jnp.abs(t[p][p]) + length[p])
            pivot_inv = jnp.where(positive, pivot_inv, -pivot_inv)
            lead_inv = jnp.where(positive, -root_inv[p], root_inv[p])
            rrow = jnp.where(lane >= j, srow[p] * lead_inv, 0.0)
            r_ref[NB + j : NB + j + 1, :] = rrow
            urow = jnp.where(lane < NB, trow[p] - rrow, trow[p])
            l_ref[j : j + 1, :] = trow[p]
            turow.append(urow * pivot_inv)
            later = jnp.where(lane == j, 1.0 - pivot_inv, turow[p])
            c_ref[j : j + 1, :] = jnp.where((lane >= j) & (lane < NB), later, 0.0)
            for q in range(p + 1, BLOCK):
                g[p, q] = (t[p][q] - s[p][q] * lead_inv) * pivot_inv
            for i in range(p + 1, BLOCK):
                for q in range(p + 1, BLOCK):
                    t[i][q] = t[i][q] - t[i][p] * g[p, q]
                trow[i] = trow[i] - t[i][p] * turow[p]
        for m in range((j0 + BLOCK) // 8, 8):
            sc, tc = [], []
            for p in range(BLOCK):
                sp, tp = S[m][:, j0 + p : j0 + p + 1], T[m][:, j0 + p : j0 + p + 1]
                sp, tp = jnp.broadcast_to(sp, (8, 128)), jnp.broadcast_to(tp, (8, 128))
                for i in range(p):
                    sp = sp - sc[i] * f[i, p]
                    tp = tp - tc[i] * g[i, p]
                sc.append(sp)
                tc.append(tp)
            for p in range(BLOCK):
                S[m] = S[m] - sc[p] * surow[p]
                T[m] = T[m] - tc[p] * turow[p]


def invert(c_ref):
    lanes = lax.broadcasted_iota(jnp.int32, (8, 128), 1)
    subs = lax.broadcasted_iota(jnp.int32, (8, 128), 0)
    C = [jnp.where(lanes == subs + 8 * b, 1.0, 0.0) for b in range(8)]
    for j0 in range(0, NB, BLOCK):
        rows = [c_ref[j0 + p : j0 + p + 1, :] for p in range(BLOCK)]
        g = {(i, p): jnp.broadcast_to(rows[i][:, j0 + p : j0 + p + 1], (1, 128)) for p in range(BLOCK) for i in range(p)}
        for m in range(j0 // 8 + 1):
            cols = []
            for p in range(BLOCK):
                col = jnp.broadcast_to(C[m][:, j0 + p : j0 + p + 1], (8, 128))
                for i in range(p):
                    col = col - cols[i] * g[i, p]
                cols.append(col)
            for p in range(BLOCK):
                C[m] = C[m] - cols[p] * rows[p]
    return stack(C)


def kernel(
    a_hbm, a_v, x_out, z_out, vt_out,
    a_hi, a_lo, head, lead, panel, prow, qpiece, dbuf, sbuf, rbuf, pbuf, wbuf, wrow, gbuf, gt_ref, cbuf, r_ref, c_ref, l_ref,
    load_sem, send, recv,
):
    r, x = lax.axis_index("row"), lax.axis_index("col")
    z, y, k = r // 8, lax.rem(r // 2, SIDE), lax.rem(r, 2)
    w = (1 - k) * z + k * y
    u = (1 - k) * y + k * z
    lanes64 = lax.broadcasted_iota(jnp.int32, (NB, 128), 1)

    def dev(z_, y_, k_, x_):
        return (z_ * 8 + y_ * 2 + k_, x_)

    def dev_w(d):
        return dev(wrap(z + d * (1 - k)), wrap(y + d * k), k, x)

    def dev_u(d):
        return dev(wrap(z + d * k), wrap(y + d * (1 - k)), k, x)

    def remote(src, dst, s, t, device):
        return pltpu.make_async_remote_copy(
            src_ref=src, dst_ref=dst, send_sem=send.at[s], recv_sem=recv.at[t],
            device_id=device, device_id_type=MESH,
        )

    sends = []

    def launch(copy, when=None):
        if when is None:
            copy.start()
        else:
            pl.when(when)(copy.start)
        sends.append((copy, when))

    def finish():
        for copy, when in sends:
            if when is None:
                copy.wait_send()
            else:
                pl.when(when)(copy.wait_send)
        sends.clear()

    sibling = dev(z, y, 1 - k, x)

    def came(dst, slot):
        remote(dst, dst, slot, slot, sibling).wait_recv()

    owns = x == 0
    first_row = r == 0
    first_chip = r < 2
    half = a_v.shape[0] // 2

    def head_load(q):
        rows = pl.ds(q * 128, 128)
        return pltpu.make_async_copy(a_hbm.at[rows, pl.ds(0, 128)], head.at[rows], load_sem.at[q])

    def load(i):
        rows = pl.ds(i * half, half)
        return pltpu.make_async_copy(a_hbm.at[rows], a_v.at[rows], load_sem.at[4 + i])

    lead_load = pltpu.make_async_copy(a_hbm.at[pl.ds(0, NB)], lead, load_sem.at[6])

    @pl.when(owns)
    def _():
        for q in range(SIDE):
            head_load(q).start()

    pl.when(first_row)(lead_load.start)
    barrier = pltpu.get_barrier_semaphore()
    peers = [dev(wrap(z + i), y, k, wrap(x + j)) for i in range(SIDE) for j in range(1, SIDE)]
    peers += [dev(wrap(z + i), wrap(y + j), k, x) for i, j in AROUND] + [sibling]
    peers += [dev(z, y, 1 - k, wrap(x + j)) for j in range(1, SIDE)]
    for peer in peers:
        pl.semaphore_signal(barrier, inc=1, device_id=peer, device_id_type=MESH)

    @pl.when((k == 1) & (r != 1))
    def _():
        pl.semaphore_signal(barrier, inc=1, device_id=dev(0, 0, 0, x), device_id_type=MESH)

    load(0).start()
    load(1).start()
    r_ref[0:NB, :] = jnp.zeros((NB, 128), jnp.float32)

    @pl.when(owns)
    def _():
        for q in range(SIDE):
            head_load(q).wait()
            panel[q] = jnp.transpose(head[q * 128 : (q + 1) * 128, :])
            if q == 0:
                panel[0, 0:NB] = jnp.where(first_row & (lanes64 < NB), 0.0, panel[0, 0:NB])
            prow[:, q * 128 : (q + 1) * 128] = panel[q, 0:NB]

    @pl.when(first_row)
    def _():
        lead_load.wait()
        lead[:, 0:128] = jnp.where(owns & (lanes64 < NB), 0.0, lead[:, 0:128])
        gram = jnp.zeros((3 * NB, 3 * NB), jnp.float32)
        for m in range(8):
            three = stack(split3(lead[:, m * 512 : (m + 1) * 512]))
            gram = gram + dot16(three, three, NT)
        gram = gram[:NB] + gram[NB : 2 * NB] + gram[2 * NB :]
        gram = gram[:, :NB] + gram[:, NB : 2 * NB] + gram[:, 2 * NB :]
        top = jnp.where(owns, lead[:, 0:128], 0.0)
        gbuf[x] = jnp.where(lanes64 < NB, jnp.concatenate([gram, gram], axis=1), top)

    def split_rows(part_id):
        load(part_id).wait()

        def body(step, carry):
            rows = pl.ds(pl.multiple_of(part_id * half + step * 16, 16), 16)
            for kk in range(2):
                for i in range(SIDE):
                    first = i * 1024 + kk * 512
                    a_hi[kk, i, rows, :], a_lo[kk, i, rows, :] = split(a_v[rows, first : first + 512])
            return carry

        lax.fori_loop(0, half // 16, body, 0)

    @pl.when(first_chip)
    def _():
        split_rows(0)
        split_rows(1)

    @pl.when(first_row)
    def _():
        pl.semaphore_wait(barrier, len(peers) + SIDE * SIDE - 1)

    @pl.when(jnp.logical_not(first_row))
    def _():
        pl.semaphore_wait(barrier, len(peers))


    for d in (2, 1, 3):
        launch(remote(prow, prow, ROWS + d, ROWS, dev(z, y, k, d)), owns)
    diagonal = x == z
    off_diagonal = jnp.logical_not(diagonal)

    def home_q(q):
        return remote(panel.at[q, pl.ds(NB, NB)], qpiece, HOME_Q + q, HOME_Q, dev(q, y, k, z))

    self_home = owns & (z == 0)
    home_local = pltpu.make_async_copy(panel.at[0, pl.ds(NB, NB)], qpiece, load_sem.at[7])

    def exchanged(buf, base):
        for d in range(1, SIDE):
            came(buf.at[wrap(x + SIDE - d)], base + d)
        return (buf[0] + buf[1]) + (buf[2] + buf[3])

    def own_piece():
        pbuf[0, 0, 0] = lead[:, 0:128]

    for d in (2, 1, 3):
        for kk in range(2):
            slot = GRAM + 2 * d + kk
            launch(remote(gbuf.at[x], gbuf.at[x], slot, GRAM + d, dev(0, 0, kk, wrap(x + d))), first_row)
    launch(remote(gbuf.at[x], gbuf.at[x], GRAM, GRAM, sibling), first_row)

    pl.when(first_row)(own_piece)
    for i, j in AROUND + [(0, 0)]:
        for kk in range(2):
            if i or j or kk:
                there = pbuf.at[kk, i if kk else j, j if kk else i]
                piece = lead.at[:, pl.ds(j * 1024 + kk * 512 + i * 128, 128)]
                launch(remote(piece, there, HOME_P + kk * 16 + i * SIDE + j, HOME_P, dev(i, j, kk, x)), first_row)

    @pl.when(jnp.logical_not(first_chip))
    def _():
        split_rows(0)
        split_rows(1)

    pl.when(r == 1)(remote(gbuf.at[x], gbuf.at[x], GRAM, GRAM, sibling).wait_recv)

    @pl.when(first_chip)
    def _():
        gt_ref[...] = exchanged(gbuf, GRAM)

    def gt_came():
        came(gt_ref, SPREAD)

    for i, j in AROUND:
        launch(remote(gt_ref, gt_ref, SPREAD + 4 * i + j, SPREAD, dev(wrap(z + i), wrap(y + j), k, x)), first_chip)

    pl.when(jnp.logical_not(owns))(remote(prow, prow, ROWS, ROWS, sibling).wait_recv)
    both = stack(split(prow[...]))

    def multiply(kk, i):
        new = dot16(both, a_hi[kk, i]) + dot16(both, a_lo[kk, i])
        return new[:NB] + new[NB:]

    for i in RING:
        j = wrap(y + i)
        new = multiply(1 - k, j)
        for q in range(SIDE):
            dbuf[1 - k, j, q] = new[:, q * 128 : (q + 1) * 128]
        launch(remote(dbuf.at[1 - k, j], sbuf.at[j], HALVES + i, HALVES + i, sibling))

    pl.when(jnp.logical_not(first_row))(remote(pbuf.at[k, u, w], pbuf.at[k, u, w], HOME_P, HOME_P, sibling).wait_recv)
    for d in (2, 1, 3):
        launch(remote(pbuf.at[k, u, w], pbuf.at[k, u, w], GATHER_P + d - 1, GATHER_P + d - 1, dev_w(d)))

    for i in RING:
        j = wrap(y + i)
        new = multiply(k, j)
        came(sbuf.at[j], HALVES + i)
        for q in range(SIDE):
            dbuf[k, j, q] = new[:, q * 128 : (q + 1) * 128] + sbuf[j, q]
        for h in RING:
            if h or i:
                q = wrap(z + h)
                slot = SCATTER + 4 * h + i
                launch(remote(dbuf.at[k, j, q], rbuf.at[4 * h + i], slot, slot, dev(q, j, k, x)))

    pl.when(self_home)(home_local.start)
    launch(home_q(0), owns & (z != 0))
    for q in range(1, SIDE):
        launch(home_q(q), owns)

    def sibling_send(buf, i, slot):
        launch(remote(buf.at[k, i], buf.at[k, i], slot, slot, sibling))

    for d in (1, 3, 2):
        came(pbuf.at[k, u, wrap(w + SIDE - d)], GATHER_P + d - 1)
    for d in (2, 1, 3):
        launch(remote(pbuf.at[k, u], pbuf.at[k, u], GATHER_P + 2 + d, GATHER_P + 2 + d, dev_u(d)))
    pl.when(jnp.logical_not(first_chip))(gt_came)
    factor(gt_ref[...], r_ref, c_ref, l_ref)
    r_all = r_ref[...]
    r_shift = jnp.transpose(r_all)[:NB, :]
    l_inv = l_ref[:, NB:]
    k_t = -dot(l_inv, r_all[NB:, NB:])

    pl.when(self_home)(home_local.wait)
    pl.when(jnp.logical_not(self_home))(remote(qpiece, qpiece, HOME_Q, HOME_Q, sibling).wait_recv)
    early = dot(l_inv, qpiece[...])
    k_p = dot(k_t, pbuf[k, u, w] - jnp.where(first_row & owns, r_shift, 0.0))
    total = dbuf[k, y, z]
    for slot in range(1, 16):
        came(rbuf.at[slot], SCATTER + slot)
        total = total + rbuf[slot]
    wbuf[k, y, z] = early + dot(k_t, total)
    for i, j in AROUND:
        slot = GATHER_W + 4 * i + j
        launch(remote(wbuf.at[k, y, z], wbuf.at[k, y, z], slot, slot, dev(wrap(z + i), wrap(y + j), k, x)))

    corner = dot(k_p, wbuf[k, y, z], NT)
    mine = 4 * k + x
    cbuf[mine] = jnp.concatenate([corner[: NB // 2], corner[NB // 2 :]], axis=1)
    for d in (2, 1, 3):
        for kk in range(2):
            slot = CORNER + 2 * d + kk
            launch(remote(cbuf.at[mine], cbuf.at[mine], slot, slot, dev(z, y, wrap_core(k + kk), wrap(x + d))))
    launch(remote(cbuf.at[mine], cbuf.at[mine], CORNER + 1, CORNER + 1, sibling))

    rows_local = pltpu.make_async_copy(wbuf.at[k, y, z], wrow.at[z], load_sem.at[8])

    def rows_copy(d):
        return remote(wbuf.at[k, y, z], wrow.at[z], OWN_ROWS + d, OWN_ROWS + z, dev(x, y, k, wrap(x + d)))

    pl.when(diagonal)(rows_local.start)
    launch(rows_copy(0), off_diagonal)
    for d in (2, 1, 3):
        launch(rows_copy(d))

    m_all = invert(c_ref)

    came(cbuf.at[4 * wrap_core(k + 1) + x], CORNER + 1)
    for d in range(1, SIDE):
        for kk in range(2):
            came(cbuf.at[4 * wrap_core(k + kk) + wrap(x + SIDE - d)], CORNER + 2 * d + kk)
    corner = cbuf[0]
    for i in range(1, 8):
        corner = corner + cbuf[i]
    cbuf[8] = corner
    for i, j in AROUND:
        slot = 4 * i + j
        launch(remote(cbuf.at[8], cbuf.at[8 + slot], CORNER_P + slot, CORNER_P + slot, dev(wrap(z + i), wrap(y + j), k, x)))

    mt = jnp.transpose(stack([m_all, jnp.zeros_like(m_all)]))[:NB, :NB]
    mt_hi, mt_lo = split(mt)
    shift = jnp.where(first_row, r_shift, 0.0)
    v_t = dot(mt, jnp.concatenate([prow[:, :128] - shift, prow[:, 128:]], axis=1))
    vt_out[...] = v_t
    shift = jnp.where(owns, r_shift, 0.0)

    def put(row, cols, hi, lo):
        z_out[row : row + NB, cols] = hi
        z_out[row + 2 * NB : row + 3 * NB, cols] = hi
        z_out[row + 4 * NB : row + 5 * NB, cols] = lo

    def make_v(kk, i):
        piece = jnp.concatenate([pbuf[kk, i, j] for j in range(SIDE)], axis=1)
        lead_shift = jnp.where((kk == 0) & (i == 0), shift, 0.0)
        hi, lo = split(jnp.concatenate([piece[:, :128] - lead_shift, piece[:, 128:]], axis=1))
        hi, lo = split((dot16(mt_lo, hi) + dot16(mt_hi, lo)) + dot16(mt_hi, hi))
        for j in range(SIDE):
            first = (1 - kk) * (i * 1024 + j * 128) + kk * (j * 1024 + 512 + i * 128)
            here = slice(j * 128, (j + 1) * 128)
            put(NB, pl.ds(pl.multiple_of(first, 128), 128), hi[:, here], lo[:, here])

    sibling_send(pbuf, u, GATHER_P + 6)
    for d in (1, 3, 2):
        came(pbuf.at[k, wrap(u + SIDE - d)], GATHER_P + 2 + d)
        sibling_send(pbuf, wrap(u + SIDE - d), GATHER_P + 6 + d)
    for d in range(SIDE):
        make_v(k, wrap(u + SIDE - d))
    for d in range(SIDE):
        came(pbuf.at[1 - k, wrap(w + SIDE - d)], GATHER_P + 6 + d)
        make_v(1 - k, wrap(w + SIDE - d))

    def use_w(kk, i):
        hi, lo = split(jnp.concatenate([wbuf[kk, i, q] for q in range(SIDE)], axis=1))
        put(0, pl.ds(pl.multiple_of(i * 1024 + kk * 512, 512), 512), hi, lo)

    for j in (0, 1, 3, 2):
        for i in (0, 1, 3, 2):
            if i or j:
                came(wbuf.at[k, wrap(y + SIDE - j), wrap(z + SIDE - i)], GATHER_W + i * SIDE + j)
        sibling_send(wbuf, wrap(y + SIDE - j), GATHER_W + 16 + j)
    for j in RING:
        use_w(k, wrap(y + SIDE - j))
    for j in (0, 1, 3, 2):
        came(wbuf.at[1 - k, wrap(y + SIDE - j)], GATHER_W + 16 + j)
        use_w(1 - k, wrap(y + SIDE - j))

    def own_came():
        for d in range(1, SIDE):
            q = wrap(z + d)
            came(wrow.at[q], OWN_ROWS + q)
        pl.when(diagonal)(rows_local.wait)
        pl.when(off_diagonal)(remote(wrow.at[z], wrow.at[z], OWN_ROWS, OWN_ROWS + z, sibling).wait_recv)

    own_came()
    w_t = jnp.concatenate([wrow[q] for q in range(SIDE)], axis=1)
    finish()
    corner = cbuf[8]
    for slot in range(1, 16):
        came(cbuf.at[8 + slot], CORNER_P + slot)
        corner = corner + cbuf[8 + slot]
    w_t = w_t - dot(stack([corner[:, :NB], corner[:, NB:]]), v_t)
    x_hi, x_lo = split(jnp.transpose(stack([v_t, w_t])))
    x_out[...] = jnp.concatenate([x_hi, x_lo, x_hi], axis=1)
    finish()


def update_kernel(a_ref, x_ref, z_ref, v_ref, out_hbm, v_hbm, buf, sem):
    parts, _, width = buf.shape
    v_copy = pltpu.make_async_copy(v_ref, v_hbm, sem.at[parts])
    v_copy.start()
    copies = []
    for i in range(parts):
        cols = slice(i * width, (i + 1) * width)
        buf[i] = a_ref[:, cols] - dot16(x_ref[...], z_ref[:, cols])
        copies.append(pltpu.make_async_copy(buf.at[i], out_hbm.at[:, pl.ds(i * width, width)], sem.at[i]))
        copies[i].start()
    for copy in copies:
        copy.wait()
    v_copy.wait()


def local(trailing):
    rows, cols = trailing.shape
    f32, b16 = jnp.float32, jnp.bfloat16
    vmem = pl.BlockSpec(memory_space=pltpu.VMEM)
    pieces = pltpu.VMEM((2, SIDE, SIDE, NB, 128), f32)
    square = pltpu.VMEM((SIDE, NB, 128), f32)
    a_copy, x_mat, z_mat, v_t = pl.pallas_call(
        kernel,
        out_shape=(
            jax.ShapeDtypeStruct((rows, cols), f32),
            jax.ShapeDtypeStruct((rows, 6 * NB), b16),
            jax.ShapeDtypeStruct((6 * NB, cols), b16),
            jax.ShapeDtypeStruct((NB, rows), f32),
        ),
        in_specs=[pl.BlockSpec(memory_space=pl.ANY)],
        out_specs=(vmem, vmem, vmem, vmem),
        scratch_shapes=[
            pltpu.VMEM((2, SIDE, rows, 512), b16),
            pltpu.VMEM((2, SIDE, rows, 512), b16),
            pltpu.VMEM((rows, 128), f32),
            pltpu.VMEM((NB, cols), f32),
            pltpu.VMEM((SIDE, 128, 128), f32),
            pltpu.VMEM((NB, rows), f32),
            pltpu.VMEM((NB, 128), f32),
            pieces,
            pltpu.VMEM((SIDE, SIDE, NB, 128), f32),
            pltpu.VMEM((SIDE * SIDE, NB, 128), f32),
            pieces,
            pieces,
            square,
            square,
            pltpu.VMEM((NB, 128), f32),
            pltpu.VMEM((6 * SIDE, NB // 2, 128), f32),
            pltpu.VMEM((128, 128), f32),
            pltpu.VMEM((NB, 128), f32),
            pltpu.VMEM((NB, 128), f32),
            pltpu.SemaphoreType.DMA((9,)),
            pltpu.SemaphoreType.DMA((COUNT,)),
            pltpu.SemaphoreType.DMA((COUNT,)),
        ],
        compiler_params=pltpu.CompilerParams(
            collective_id=0, has_side_effects=True, vmem_limit_bytes=38 * 2**20
        ),
    )(trailing)
    step = 512
    hbm = pl.BlockSpec(memory_space=pl.ANY)
    reduced, v_t = pl.pallas_call(
        update_kernel,
        out_shape=(jax.ShapeDtypeStruct((rows, cols), f32), jax.ShapeDtypeStruct((NB, rows), f32)),
        in_specs=[vmem, vmem, vmem, vmem],
        out_specs=(hbm, hbm),
        scratch_shapes=[pltpu.VMEM((cols // step, rows, step), f32), pltpu.SemaphoreType.DMA((cols // step + 1,))],
        compiler_params=pltpu.CompilerParams(vmem_limit_bytes=24 * 2**20),
    )(a_copy, x_mat, z_mat, v_t)
    return reduced, v_t.T


def solution(mesh):
    return jax.shard_map(
        local, mesh=mesh, in_specs=(P("row", "col"),), out_specs=(P("row", "col"), P("row", None)), check_vma=False
    )
```

```python
import jax
import jax.numpy as jnp
from jax import lax
from jax.experimental import pallas as pl
from jax.experimental.pallas import tpu as pltpu
from jax.sharding import PartitionSpec as P

NB = 64
BLOCK = 8
SIDE = 4
MESH = pl.DeviceIdType.MESH
HIGHEST = lax.Precision.HIGHEST
NN = (((1,), (0,)), ((), ()))
NT = (((1,), (1,)), ((), ()))
TN = (((0,), (0,)), ((), ()))


def dot(a, b, dims=NN):
    return lax.dot_general(a, b, dims, precision=HIGHEST, preferred_element_type=jnp.float32)


def dot16(a, b, dims=NN):
    return lax.dot_general(a, b, dims, preferred_element_type=jnp.float32)


def split(a):
    high = a.astype(jnp.bfloat16)
    return high, (a - high.astype(jnp.float32)).astype(jnp.bfloat16)


def split3(a):
    high = a.astype(jnp.bfloat16)
    rest = a - high.astype(jnp.float32)
    middle = rest.astype(jnp.bfloat16)
    return high, middle, (rest - middle.astype(jnp.float32)).astype(jnp.bfloat16)


def stack(parts):
    return jnp.concatenate(parts, axis=0)


def wrap(i):
    return i & (SIDE - 1)


def wrap_core(i):
    return i & 1


AROUND = [(2, 2), (2, 1), (2, 3), (1, 2), (3, 2), (1, 1), (3, 3), (1, 3), (3, 1), (2, 0), (0, 2), (1, 0), (3, 0), (0, 1), (0, 3)]


RING = (2, 1, 3, 0)


class Ids:
    def __init__(self):
        self.count = 0

    def take(self, n):
        first = self.count
        self.count += n
        return first


IDS = Ids()
ROWS = IDS.take(4)
HOME_P = IDS.take(32)
HOME_Q = IDS.take(4)
GRAM = IDS.take(8)
SPREAD = IDS.take(17)
HALVES = IDS.take(4)
SCATTER = IDS.take(16)
GATHER_P = IDS.take(10)
GATHER_W = IDS.take(20)
OWN_ROWS = IDS.take(4)
CORNER = IDS.take(8)
CORNER_P = IDS.take(16)
COUNT = IDS.count


def factor(gt, r_ref, c_ref, l_ref):
    lanes = lax.broadcasted_iota(jnp.int32, (8, 128), 1)
    subs = lax.broadcasted_iota(jnp.int32, (8, 128), 0)
    lane = lax.broadcasted_iota(jnp.int32, (1, 128), 1)
    t_all = jnp.transpose(stack([gt, jnp.zeros_like(gt)]))[NB:, :]
    S, T = [], []
    for b in range(8):
        rows = slice(8 * b, 8 * b + 8)
        unit = jnp.where(lanes == subs + (8 * b + NB), 1.0, 0.0)
        S.append(jnp.where(lanes < NB, gt[rows], unit))
        T.append(jnp.where(lanes < NB, t_all[rows], unit))

    def spread(row, j):
        return jnp.broadcast_to(row[:, j : j + 1], (1, 128))

    for j0 in range(0, NB, BLOCK):
        b, s0 = j0 // 8, j0 % 8
        srow = [S[b][s0 + p : s0 + p + 1, :] for p in range(BLOCK)]
        trow = [T[b][s0 + p : s0 + p + 1, :] for p in range(BLOCK)]
        s = [[spread(srow[p], j0 + q) if q >= p else None for q in range(BLOCK)] for p in range(BLOCK)]
        t = [[spread(trow[p], j0 + q) for q in range(BLOCK)] for p in range(BLOCK)]
        d_inv, root_inv, length, f = [], [], [], {}
        for p in range(BLOCK):
            d_inv.append(1.0 / s[p][p])
            root_inv.append(lax.rsqrt(s[p][p]))
            length.append(s[p][p] * root_inv[p])
            for i in range(p + 1, BLOCK):
                f[p, i] = s[p][i] * d_inv[p]
                for q in range(i, BLOCK):
                    s[i][q] = s[i][q] - f[p, i] * s[p][q]
                srow[i] = srow[i] - f[p, i] * srow[p]
        surow = [srow[p] * d_inv[p] for p in range(BLOCK)]
        turow, g = [], {}
        for p in range(BLOCK):
            j = j0 + p
            positive = t[p][p] >= 0.0
            pivot_inv = 1.0 / (jnp.abs(t[p][p]) + length[p])
            pivot_inv = jnp.where(positive, pivot_inv, -pivot_inv)
            lead_inv = jnp.where(positive, -root_inv[p], root_inv[p])
            rrow = jnp.where(lane >= j, srow[p] * lead_inv, 0.0)
            r_ref[NB + j : NB + j + 1, :] = rrow
            urow = jnp.where(lane < NB, trow[p] - rrow, trow[p])
            l_ref[j : j + 1, :] = trow[p]
            turow.append(urow * pivot_inv)
            later = jnp.where(lane == j, 1.0 - pivot_inv, turow[p])
            c_ref[j : j + 1, :] = jnp.where((lane >= j) & (lane < NB), later, 0.0)
            for q in range(p + 1, BLOCK):
                g[p, q] = (t[p][q] - s[p][q] * lead_inv) * pivot_inv
            for i in range(p + 1, BLOCK):
                for q in range(p + 1, BLOCK):
                    t[i][q] = t[i][q] - t[i][p] * g[p, q]
                trow[i] = trow[i] - t[i][p] * turow[p]
        for m in range((j0 + BLOCK) // 8, 8):
            sc, tc = [], []
            for p in range(BLOCK):
                sp, tp = S[m][:, j0 + p : j0 + p + 1], T[m][:, j0 + p : j0 + p + 1]
                sp, tp = jnp.broadcast_to(sp, (8, 128)), jnp.broadcast_to(tp, (8, 128))
                for i in range(p):
                    sp = sp - sc[i] * f[i, p]
                    tp = tp - tc[i] * g[i, p]
                sc.append(sp)
                tc.append(tp)
            for p in range(BLOCK):
                S[m] = S[m] - sc[p] * surow[p]
                T[m] = T[m] - tc[p] * turow[p]


def invert(c_ref):
    lanes = lax.broadcasted_iota(jnp.int32, (8, 128), 1)
    subs = lax.broadcasted_iota(jnp.int32, (8, 128), 0)
    C = [jnp.where(lanes == subs + 8 * b, 1.0, 0.0) for b in range(8)]
    for j0 in range(0, NB, BLOCK):
        rows = [c_ref[j0 + p : j0 + p + 1, :] for p in range(BLOCK)]
        g = {(i, p): jnp.broadcast_to(rows[i][:, j0 + p : j0 + p + 1], (1, 128)) for p in range(BLOCK) for i in range(p)}
        for m in range(j0 // 8 + 1):
            cols = []
            for p in range(BLOCK):
                col = jnp.broadcast_to(C[m][:, j0 + p : j0 + p + 1], (8, 128))
                for i in range(p):
                    col = col - cols[i] * g[i, p]
                cols.append(col)
            for p in range(BLOCK):
                C[m] = C[m] - cols[p] * rows[p]
    return stack(C)


def kernel(
    a_hbm, a_v, x_out, z_out, vt_out,
    a_hi, a_lo, head, lead, panel, prow, qpiece, dbuf, sbuf, rbuf, pbuf, wbuf, wrow, gbuf, gt_ref, cbuf, r_ref, c_ref, l_ref,
    load_sem, send, recv,
):
    r, x = lax.axis_index("row"), lax.axis_index("col")
    z, y, k = r // 8, lax.rem(r // 2, SIDE), lax.rem(r, 2)
    w = (1 - k) * z + k * y
    u = (1 - k) * y + k * z
    lanes64 = lax.broadcasted_iota(jnp.int32, (NB, 128), 1)

    def dev(z_, y_, k_, x_):
        return (z_ * 8 + y_ * 2 + k_, x_)

    def dev_w(d):
        return dev(wrap(z + d * (1 - k)), wrap(y + d * k), k, x)

    def dev_u(d):
        return dev(wrap(z + d * k), wrap(y + d * (1 - k)), k, x)

    def remote(src, dst, s, t, device):
        return pltpu.make_async_remote_copy(
            src_ref=src, dst_ref=dst, send_sem=send.at[s], recv_sem=recv.at[t],
            device_id=device, device_id_type=MESH,
        )

    sends = []

    def launch(copy, when=None):
        if when is None:
            copy.start()
        else:
            pl.when(when)(copy.start)
        sends.append((copy, when))

    def finish():
        for copy, when in sends:
            if when is None:
                copy.wait_send()
            else:
                pl.when(when)(copy.wait_send)
        sends.clear()

    sibling = dev(z, y, 1 - k, x)

    def came(dst, slot):
        remote(dst, dst, slot, slot, sibling).wait_recv()

    owns = x == 0
    first_row = r == 0
    first_chip = r < 2
    half = a_v.shape[0] // 2

    def head_load(q):
        rows = pl.ds(q * 128, 128)
        return pltpu.make_async_copy(a_hbm.at[rows, pl.ds(0, 128)], head.at[rows], load_sem.at[q])

    def load(i):
        rows = pl.ds(i * half, half)
        return pltpu.make_async_copy(a_hbm.at[rows], a_v.at[rows], load_sem.at[4 + i])

    lead_load = pltpu.make_async_copy(a_hbm.at[pl.ds(0, NB)], lead, load_sem.at[6])

    @pl.when(owns)
    def _():
        for q in range(SIDE):
            head_load(q).start()

    pl.when(first_row)(lead_load.start)
    barrier = pltpu.get_barrier_semaphore()
    peers = [dev(wrap(z + i), y, k, wrap(x + j)) for i in range(SIDE) for j in range(1, SIDE)]
    peers += [dev(wrap(z + i), wrap(y + j), k, x) for i, j in AROUND] + [sibling]
    peers += [dev(z, y, 1 - k, wrap(x + j)) for j in range(1, SIDE)]
    for peer in peers:
        pl.semaphore_signal(barrier, inc=1, device_id=peer, device_id_type=MESH)

    @pl.when((k == 1) & (r != 1))
    def _():
        pl.semaphore_signal(barrier, inc=1, device_id=dev(0, 0, 0, x), device_id_type=MESH)

    load(0).start()
    load(1).start()
    r_ref[0:NB, :] = jnp.zeros((NB, 128), jnp.float32)

    @pl.when(owns)
    def _():
        for q in range(SIDE):
            head_load(q).wait()
            panel[q] = jnp.transpose(head[q * 128 : (q + 1) * 128, :])
            if q == 0:
                panel[0, 0:NB] = jnp.where(first_row & (lanes64 < NB), 0.0, panel[0, 0:NB])
            prow[:, q * 128 : (q + 1) * 128] = panel[q, 0:NB]

    @pl.when(first_row)
    def _():
        lead_load.wait()
        lead[:, 0:128] = jnp.where(owns & (lanes64 < NB), 0.0, lead[:, 0:128])
        gram = jnp.zeros((3 * NB, 3 * NB), jnp.float32)
        for m in range(8):
            three = stack(split3(lead[:, m * 512 : (m + 1) * 512]))
            gram = gram + dot16(three, three, NT)
        gram = gram[:NB] + gram[NB : 2 * NB] + gram[2 * NB :]
        gram = gram[:, :NB] + gram[:, NB : 2 * NB] + gram[:, 2 * NB :]
        top = jnp.where(owns, lead[:, 0:128], 0.0)
        gbuf[x] = jnp.where(lanes64 < NB, jnp.concatenate([gram, gram], axis=1), top)

    def split_rows(part_id):
        load(part_id).wait()

        def body(step, carry):
            rows = pl.ds(pl.multiple_of(part_id * half + step * 16, 16), 16)
            for kk in range(2):
                for i in range(SIDE):
                    first = i * 1024 + kk * 512
                    a_hi[kk, i, rows, :], a_lo[kk, i, rows, :] = split(a_v[rows, first : first + 512])
            return carry

        lax.fori_loop(0, half // 16, body, 0)

    @pl.when(first_chip)
    def _():
        split_rows(0)
        split_rows(1)

    @pl.when(first_row)
    def _():
        pl.semaphore_wait(barrier, len(peers) + SIDE * SIDE - 1)

    @pl.when(jnp.logical_not(first_row))
    def _():
        pl.semaphore_wait(barrier, len(peers))


    for d in (2, 1, 3):
        launch(remote(prow, prow, ROWS + d, ROWS, dev(z, y, k, d)), owns)
    diagonal = x == z
    off_diagonal = jnp.logical_not(diagonal)

    def home_q(q):
        return remote(panel.at[q, pl.ds(NB, NB)], qpiece, HOME_Q + q, HOME_Q, dev(q, y, k, z))

    self_home = owns & (z == 0)
    home_local = pltpu.make_async_copy(panel.at[0, pl.ds(NB, NB)], qpiece, load_sem.at[7])

    def exchanged(buf, base):
        for d in range(1, SIDE):
            came(buf.at[wrap(x + SIDE - d)], base + d)
        return (buf[0] + buf[1]) + (buf[2] + buf[3])

    def own_piece():
        pbuf[0, 0, 0] = lead[:, 0:128]

    for d in (2, 1, 3):
        for kk in range(2):
            slot = GRAM + 2 * d + kk
            launch(remote(gbuf.at[x], gbuf.at[x], slot, GRAM + d, dev(0, 0, kk, wrap(x + d))), first_row)
    launch(remote(gbuf.at[x], gbuf.at[x], GRAM, GRAM, sibling), first_row)

    pl.when(first_row)(own_piece)
    for i, j in AROUND + [(0, 0)]:
        for kk in range(2):
            if i or j or kk:
                there = pbuf.at[kk, i if kk else j, j if kk else i]
                piece = lead.at[:, pl.ds(j * 1024 + kk * 512 + i * 128, 128)]
                launch(remote(piece, there, HOME_P + kk * 16 + i * SIDE + j, HOME_P, dev(i, j, kk, x)), first_row)

    @pl.when(jnp.logical_not(first_chip))
    def _():
        split_rows(0)
        split_rows(1)

    pl.when(r == 1)(remote(gbuf.at[x], gbuf.at[x], GRAM, GRAM, sibling).wait_recv)

    @pl.when(first_chip)
    def _():
        gt_ref[...] = exchanged(gbuf, GRAM)

    def gt_came():
        came(gt_ref, SPREAD)

    for i, j in AROUND:
        launch(remote(gt_ref, gt_ref, SPREAD + 4 * i + j, SPREAD, dev(wrap(z + i), wrap(y + j), k, x)), first_chip)

    pl.when(jnp.logical_not(owns))(remote(prow, prow, ROWS, ROWS, sibling).wait_recv)
    both = stack(split(prow[...]))

    def multiply(kk, i):
        new = dot16(both, a_hi[kk, i]) + dot16(both, a_lo[kk, i])
        return new[:NB] + new[NB:]

    for i in RING:
        j = wrap(y + i)
        new = multiply(1 - k, j)
        for q in range(SIDE):
            dbuf[1 - k, j, q] = new[:, q * 128 : (q + 1) * 128]
        launch(remote(dbuf.at[1 - k, j], sbuf.at[j], HALVES + i, HALVES + i, sibling))

    pl.when(jnp.logical_not(first_row))(remote(pbuf.at[k, u, w], pbuf.at[k, u, w], HOME_P, HOME_P, sibling).wait_recv)
    for d in (2, 1, 3):
        launch(remote(pbuf.at[k, u, w], pbuf.at[k, u, w], GATHER_P + d - 1, GATHER_P + d - 1, dev_w(d)))

    for i in RING:
        j = wrap(y + i)
        new = multiply(k, j)
        came(sbuf.at[j], HALVES + i)
        for q in range(SIDE):
            dbuf[k, j, q] = new[:, q * 128 : (q + 1) * 128] + sbuf[j, q]
        for h in RING:
            if h or i:
                q = wrap(z + h)
                slot = SCATTER + 4 * h + i
                launch(remote(dbuf.at[k, j, q], rbuf.at[4 * h + i], slot, slot, dev(q, j, k, x)))

    pl.when(self_home)(home_local.start)
    launch(home_q(0), owns & (z != 0))
    for q in range(1, SIDE):
        launch(home_q(q), owns)

    def sibling_send(buf, i, slot):
        launch(remote(buf.at[k, i], buf.at[k, i], slot, slot, sibling))

    for d in (1, 3, 2):
        came(pbuf.at[k, u, wrap(w + SIDE - d)], GATHER_P + d - 1)
    for d in (2, 1, 3):
        launch(remote(pbuf.at[k, u], pbuf.at[k, u], GATHER_P + 2 + d, GATHER_P + 2 + d, dev_u(d)))
    pl.when(jnp.logical_not(first_chip))(gt_came)
    factor(gt_ref[...], r_ref, c_ref, l_ref)
    r_all = r_ref[...]
    r_shift = jnp.transpose(r_all)[:NB, :]
    l_inv = l_ref[:, NB:]
    k_t = -dot(l_inv, r_all[NB:, NB:])

    pl.when(self_home)(home_local.wait)
    pl.when(jnp.logical_not(self_home))(remote(qpiece, qpiece, HOME_Q, HOME_Q, sibling).wait_recv)
    early = dot(l_inv, qpiece[...])
    k_p = dot(k_t, pbuf[k, u, w] - jnp.where(first_row & owns, r_shift, 0.0))
    total = dbuf[k, y, z]
    for slot in range(1, 16):
        came(rbuf.at[slot], SCATTER + slot)
        total = total + rbuf[slot]
    wbuf[k, y, z] = early + dot(k_t, total)
    for i, j in AROUND:
        slot = GATHER_W + 4 * i + j
        launch(remote(wbuf.at[k, y, z], wbuf.at[k, y, z], slot, slot, dev(wrap(z + i), wrap(y + j), k, x)))

    corner = dot(k_p, wbuf[k, y, z], NT)
    mine = 4 * k + x
    cbuf[mine] = jnp.concatenate([corner[: NB // 2], corner[NB // 2 :]], axis=1)
    for d in (2, 1, 3):
        for kk in range(2):
            slot = CORNER + 2 * d + kk
            launch(remote(cbuf.at[mine], cbuf.at[mine], slot, slot, dev(z, y, wrap_core(k + kk), wrap(x + d))))
    launch(remote(cbuf.at[mine], cbuf.at[mine], CORNER + 1, CORNER + 1, sibling))

    rows_local = pltpu.make_async_copy(wbuf.at[k, y, z], wrow.at[z], load_sem.at[8])

    def rows_copy(d):
        return remote(wbuf.at[k, y, z], wrow.at[z], OWN_ROWS + d, OWN_ROWS + z, dev(x, y, k, wrap(x + d)))

    pl.when(diagonal)(rows_local.start)
    launch(rows_copy(0), off_diagonal)
    for d in (2, 1, 3):
        launch(rows_copy(d))

    m_all = invert(c_ref)

    came(cbuf.at[4 * wrap_core(k + 1) + x], CORNER + 1)
    for d in range(1, SIDE):
        for kk in range(2):
            came(cbuf.at[4 * wrap_core(k + kk) + wrap(x + SIDE - d)], CORNER + 2 * d + kk)
    corner = cbuf[0]
    for i in range(1, 8):
        corner = corner + cbuf[i]
    cbuf[8] = corner
    for i, j in AROUND:
        slot = 4 * i + j
        launch(remote(cbuf.at[8], cbuf.at[8 + slot], CORNER_P + slot, CORNER_P + slot, dev(wrap(z + i), wrap(y + j), k, x)))

    mt = jnp.transpose(stack([m_all, jnp.zeros_like(m_all)]))[:NB, :NB]
    mt_hi, mt_lo = split(mt)
    shift = jnp.where(first_row, r_shift, 0.0)
    v_t = dot(mt, jnp.concatenate([prow[:, :128] - shift, prow[:, 128:]], axis=1))
    vt_out[...] = v_t
    shift = jnp.where(owns, r_shift, 0.0)

    def put(row, cols, hi, lo):
        z_out[row : row + NB, cols] = hi
        z_out[row + 2 * NB : row + 3 * NB, cols] = hi
        z_out[row + 4 * NB : row + 5 * NB, cols] = lo

    def make_v(kk, i):
        piece = jnp.concatenate([pbuf[kk, i, j] for j in range(SIDE)], axis=1)
        lead_shift = jnp.where((kk == 0) & (i == 0), shift, 0.0)
        hi, lo = split(jnp.concatenate([piece[:, :128] - lead_shift, piece[:, 128:]], axis=1))
        hi, lo = split((dot16(mt_lo, hi) + dot16(mt_hi, lo)) + dot16(mt_hi, hi))
        for j in range(SIDE):
            first = (1 - kk) * (i * 1024 + j * 128) + kk * (j * 1024 + 512 + i * 128)
            here = slice(j * 128, (j + 1) * 128)
            put(NB, pl.ds(pl.multiple_of(first, 128), 128), hi[:, here], lo[:, here])

    sibling_send(pbuf, u, GATHER_P + 6)
    for d in (1, 3, 2):
        came(pbuf.at[k, wrap(u + SIDE - d)], GATHER_P + 2 + d)
        sibling_send(pbuf, wrap(u + SIDE - d), GATHER_P + 6 + d)
    for d in range(SIDE):
        make_v(k, wrap(u + SIDE - d))
    for d in range(SIDE):
        came(pbuf.at[1 - k, wrap(w + SIDE - d)], GATHER_P + 6 + d)
        make_v(1 - k, wrap(w + SIDE - d))

    def use_w(kk, i):
        hi, lo = split(jnp.concatenate([wbuf[kk, i, q] for q in range(SIDE)], axis=1))
        put(0, pl.ds(pl.multiple_of(i * 1024 + kk * 512, 512), 512), hi, lo)

    for j in (0, 1, 3, 2):
        for i in (0, 1, 3, 2):
            if i or j:
                came(wbuf.at[k, wrap(y + SIDE - j), wrap(z + SIDE - i)], GATHER_W + i * SIDE + j)
        sibling_send(wbuf, wrap(y + SIDE - j), GATHER_W + 16 + j)
    for j in RING:
        use_w(k, wrap(y + SIDE - j))
    for j in (0, 1, 3, 2):
        came(wbuf.at[1 - k, wrap(y + SIDE - j)], GATHER_W + 16 + j)
        use_w(1 - k, wrap(y + SIDE - j))

    def own_came():
        for d in range(1, SIDE):
            q = wrap(z + d)
            came(wrow.at[q], OWN_ROWS + q)
        pl.when(diagonal)(rows_local.wait)
        pl.when(off_diagonal)(remote(wrow.at[z], wrow.at[z], OWN_ROWS, OWN_ROWS + z, sibling).wait_recv)

    x_hi, x_lo = split(jnp.transpose(stack([v_t, v_t])))
    for part, there in ((x_hi, 0), (x_lo, 2 * NB), (x_hi, 4 * NB)):
        x_out[:, there : there + NB] = part[:, :NB]
    own_came()
    w_t = jnp.concatenate([wrow[q] for q in range(SIDE)], axis=1)
    finish()
    corner = cbuf[8]
    for slot in range(1, 16):
        came(cbuf.at[8 + slot], CORNER_P + slot)
        corner = corner + cbuf[8 + slot]
    w_t = w_t - dot(stack([corner[:, :NB], corner[:, NB:]]), v_t)
    x_hi, x_lo = split(jnp.transpose(stack([w_t, w_t])))
    for part, there in ((x_hi, NB), (x_lo, 3 * NB), (x_hi, 5 * NB)):
        x_out[:, there : there + NB] = part[:, NB:]
    finish()


def update_kernel(a_ref, x_ref, z_ref, v_ref, out_hbm, v_hbm, buf, sem):
    parts, _, width = buf.shape
    v_copy = pltpu.make_async_copy(v_ref, v_hbm, sem.at[parts])
    v_copy.start()
    copies = []
    for i in range(parts):
        cols = slice(i * width, (i + 1) * width)
        buf[i] = a_ref[:, cols] - dot16(x_ref[...], z_ref[:, cols])
        copies.append(pltpu.make_async_copy(buf.at[i], out_hbm.at[:, pl.ds(i * width, width)], sem.at[i]))
        copies[i].start()
    for copy in copies:
        copy.wait()
    v_copy.wait()


def local(trailing):
    rows, cols = trailing.shape
    f32, b16 = jnp.float32, jnp.bfloat16
    vmem = pl.BlockSpec(memory_space=pltpu.VMEM)
    pieces = pltpu.VMEM((2, SIDE, SIDE, NB, 128), f32)
    square = pltpu.VMEM((SIDE, NB, 128), f32)
    a_copy, x_mat, z_mat, v_t = pl.pallas_call(
        kernel,
        out_shape=(
            jax.ShapeDtypeStruct((rows, cols), f32),
            jax.ShapeDtypeStruct((rows, 6 * NB), b16),
            jax.ShapeDtypeStruct((6 * NB, cols), b16),
            jax.ShapeDtypeStruct((NB, rows), f32),
        ),
        in_specs=[pl.BlockSpec(memory_space=pl.ANY)],
        out_specs=(vmem, vmem, vmem, vmem),
        scratch_shapes=[
            pltpu.VMEM((2, SIDE, rows, 512), b16),
            pltpu.VMEM((2, SIDE, rows, 512), b16),
            pltpu.VMEM((rows, 128), f32),
            pltpu.VMEM((NB, cols), f32),
            pltpu.VMEM((SIDE, 128, 128), f32),
            pltpu.VMEM((NB, rows), f32),
            pltpu.VMEM((NB, 128), f32),
            pieces,
            pltpu.VMEM((SIDE, SIDE, NB, 128), f32),
            pltpu.VMEM((SIDE * SIDE, NB, 128), f32),
            pieces,
            pieces,
            square,
            square,
            pltpu.VMEM((NB, 128), f32),
            pltpu.VMEM((6 * SIDE, NB // 2, 128), f32),
            pltpu.VMEM((128, 128), f32),
            pltpu.VMEM((NB, 128), f32),
            pltpu.VMEM((NB, 128), f32),
            pltpu.SemaphoreType.DMA((9,)),
            pltpu.SemaphoreType.DMA((COUNT,)),
            pltpu.SemaphoreType.DMA((COUNT,)),
        ],
        compiler_params=pltpu.CompilerParams(
            collective_id=0, has_side_effects=True, vmem_limit_bytes=38 * 2**20
        ),
    )(trailing)
    step = 512
    hbm = pl.BlockSpec(memory_space=pl.ANY)
    reduced, v_t = pl.pallas_call(
        update_kernel,
        out_shape=(jax.ShapeDtypeStruct((rows, cols), f32), jax.ShapeDtypeStruct((NB, rows), f32)),
        in_specs=[vmem, vmem, vmem, vmem],
        out_specs=(hbm, hbm),
        scratch_shapes=[pltpu.VMEM((cols // step, rows, step), f32), pltpu.SemaphoreType.DMA((cols // step + 1,))],
        compiler_params=pltpu.CompilerParams(vmem_limit_bytes=24 * 2**20),
    )(a_copy, x_mat, z_mat, v_t)
    return reduced, v_t.T


def solution(mesh):
    return jax.shard_map(
        local, mesh=mesh, in_specs=(P("row", "col"),), out_specs=(P("row", "col"), P("row", None)), check_vma=False
    )
```
